32 devices in a mesh: shot: 4 (over y, x), blk: 8 (over z, core).
Axes of the slice: x: 2, y: 2, z: 4, core: 2. Of those that a mesh axis runs over, the one named last changes fastest.
Arguments:
- state_before: float32 [4, 64, 64, 128], P('shot', 'blk'), may hold values from -7 to 7
- state_now: float32 [4, 64, 64, 128], P('shot', 'blk'), may hold values from -7 to 7
- adjoint_later: float32 [4, 64, 64, 128], P('shot', 'blk'), may hold values from -7 to 7
- adjoint_now: float32 [4, 64, 64, 128], P('shot', 'blk'), may hold values from -7 to 7
- courant_sq: float32 [64, 128, 128], P('blk', 'shot'), may hold values from 0.02 to 0.3
- epsilon: float32 [64, 128, 128], P('blk', 'shot'), may hold values from 0.02 to 0.3
- tilt_angle: float32 [64, 128, 128], P('blk', 'shot'), may hold values from 0 to 1.2
- azimuth: float32 [64, 128, 128], P('blk', 'shot'), may hold values from -3.140625 to 3.140625
- aperture_anchor: int32 [4], P('shot'), may hold values from 0 to 64, as said below
- step_index: int32 [1], replicated, may hold values from 0 to 12
- wavelet: float32 [4, 16], P('shot'), may hold values from -8 to 8
- residual_traces: float32 [4, 16, 128], P('shot'), may hold values from -6 to 6
- source_x: int32 [4], P('shot'), may hold values from 0 to 63
- source_y: int32 [4], P('shot'), may hold values from 0 to 63
- source_z: int32 [4], P('shot'), may hold values from 0 to 127
- receiver_x: int32 [4, 128], P('shot'), may hold values from 0 to 63
- receiver_y: int32 [4, 128], P('shot'), may hold values from 0 to 63
- receiver_z: int32 [4, 128], P('shot'), may hold values from 0 to 127
Outputs:
- adjoint_one: float32 [4, 64, 64, 128], P('shot', 'blk')
- adjoint_zero: float32 [4, 64, 64, 128], P('shot', 'blk')
- model_grad: float32 [64, 128, 128], P('blk', 'shot')
The draws below stay inside these ranges and needn't reach their ends.
Inputs may be any that keep to these rules, and one draw needn't show every extreme that they name: `aperture_anchor`: each value is a multiple of 32; some shot has 0 and some shot has 64.
All inputs are finite; a program needn't handle non-finite values.
Results may differ from the reference program's by a relative error of at most 0.0003.
Values sent between devices are 32-bit elements; how exact they have to be, the bound alone decides.
No kernel may reach another device: no remote copies, remote signals or barrier semaphores. Data moves between devices by JAX's collectives and lax.ppermute only.
A program may use at most 64 MiB of HBM per device.

```python
import jax
import jax.numpy as jnp
from jax import lax

NY = 64
NZ = 128
STEPS = 4
NT = 16
NREC = 128
SHOTS = 4
AX = 64
NYG = 128
YSH = 32


def draw_aperture_anchor(key, part):
    positions = (NYG - NY) // YSH + 1
    picked = jax.random.randint(key, (SHOTS,), 0, positions)
    ordering = jax.random.permutation(jax.random.fold_in(key, 7), SHOTS)
    picked = jnp.where(ordering == 0, 0, jnp.where(ordering == 1, positions - 1, picked))
    return (picked * YSH).astype(jnp.int32)


def state_field(key, salt):
    folded = jax.random.fold_in(key, salt)
    random_part = jnp.clip(jax.random.normal(folded, (SHOTS, AX, NY, NZ), jnp.float32), -6.0, 6.0)
    return random_part.astype(jnp.float32)


def draw_state_before(key, part):
    return state_field(key, 101)


def draw_state_now(key, part):
    return state_field(key, 202)


def draw_adjoint_later(key, part):
    return state_field(key, 303)


def draw_adjoint_now(key, part):
    return state_field(key, 404)


def place_ends(values, own_key, low, top_value):
    index_at = [jax.random.randint(jax.random.fold_in(own_key, axis), (), 0, length) for axis, length in enumerate(values.shape)]
    widest = values.shape.index(max(values.shape))
    next_to = index_at[:widest] + [(index_at[widest] + 1) % values.shape[widest]] + index_at[widest + 1:]
    return values.at[tuple(index_at)].set(low).at[tuple(next_to)].set(top_value)


def levels(key, shape, pieces, low, high):
    def one(position, shards_of):
        draws = jax.random.uniform(jax.random.fold_in(jax.random.fold_in(key, 6), position), (shards_of,), jnp.float32, low / len(pieces), high / len(pieces))
        return jnp.repeat(jnp.exp(draws), shape[position] // shards_of).reshape((-1,) + (1,) * (len(shape) - position - 1))

    level = one(*pieces[0])
    for cut in pieces[1:]:
        level = level * one(*cut)
    return level


def centred(stream_key, shape, width, bound, split=(), held_as=jnp.bfloat16):
    array = width * jax.random.normal(stream_key, shape, jnp.float32)
    if split:
        array = array * levels(stream_key, shape, split, -0.22, 0.18)
    return jnp.clip(array, -bound, bound).astype(held_as)


def setup_inputs(seed: int = 0) -> dict:
    key_of = jax.random.split(jax.random.key(seed), 19)
    state_before = draw_state_before(jax.random.fold_in(key_of[18], 71), 0)
    state_now = draw_state_now(jax.random.fold_in(key_of[18], 71), 0)
    adjoint_later = draw_adjoint_later(jax.random.fold_in(key_of[18], 71), 0)
    adjoint_now = draw_adjoint_now(jax.random.fold_in(key_of[18], 71), 0)
    courant_sq = jnp.clip(0.02 + 0.28 * jax.random.uniform(key_of[4], (AX, NYG, NZ), jnp.float32) ** levels(key_of[4], (AX, NYG, NZ), ((0, 8), (1, 4)), -0.2, 0.2), 0.02, 0.3)
    epsilon = jnp.clip(0.02 + 0.28 * jax.random.uniform(key_of[5], (AX, NYG, NZ), jnp.float32) ** levels(key_of[5], (AX, NYG, NZ), ((0, 8), (1, 4)), -0.2, 0.2), 0.02, 0.3)
    tilt_angle = jnp.clip(1.2 * jax.random.uniform(key_of[6], (AX, NYG, NZ), jnp.float32) ** levels(key_of[6], (AX, NYG, NZ), ((0, 8), (1, 4)), -0.2, 0.2), 0.0, 1.2)
    azimuth = jnp.clip(jax.random.uniform(key_of[7], (AX, NYG, NZ), jnp.float32, -3.140625, 3.140625), -3.140625, 3.140625)
    aperture_anchor = draw_aperture_anchor(jax.random.fold_in(key_of[18], 71), 0)
    step_index = jax.random.randint(key_of[9], (1,), 0, NT - STEPS + 1).astype(jnp.int32)
    wavelet = centred(key_of[10], (SHOTS, NT), 2.0, 8.0, ((0, 4),), jnp.float32)
    residual_traces = centred(key_of[11], (SHOTS, NT, NREC), 1.0, 6.0, ((0, 4),), jnp.float32)
    source_x = place_ends(jax.random.randint(key_of[12], (SHOTS,), 0, AX), jax.random.fold_in(key_of[12], 1), 0, AX - 1).astype(jnp.int32)
    source_y = place_ends(jax.random.randint(key_of[13], (SHOTS,), 0, NY), jax.random.fold_in(key_of[13], 1), 0, NY - 1).astype(jnp.int32)
    source_z = place_ends(jax.random.randint(key_of[14], (SHOTS,), 0, NZ), jax.random.fold_in(key_of[14], 1), 0, NZ - 1).astype(jnp.int32)
    receiver_x = place_ends(jax.random.randint(key_of[15], (SHOTS, NREC), 0, AX), jax.random.fold_in(key_of[15], 1), 0, AX - 1).astype(jnp.int32)
    receiver_y = place_ends(jax.random.randint(key_of[16], (SHOTS, NREC), 0, NY), jax.random.fold_in(key_of[16], 1), 0, NY - 1).astype(jnp.int32)
    receiver_z = place_ends(jax.random.randint(key_of[17], (SHOTS, NREC), 0, NZ), jax.random.fold_in(key_of[17], 1), 0, NZ - 1).astype(jnp.int32)
    return {"state_before": state_before, "state_now": state_now, "adjoint_later": adjoint_later, "adjoint_now": adjoint_now, "courant_sq": courant_sq, "epsilon": epsilon, "tilt_angle": tilt_angle, "azimuth": azimuth, "aperture_anchor": aperture_anchor, "step_index": step_index, "wavelet": wavelet, "residual_traces": residual_traces, "source_x": source_x, "source_y": source_y, "source_z": source_z, "receiver_x": receiver_x, "receiver_y": receiver_y, "receiver_z": receiver_z}


COEF = (0.8, -0.2, 4.0 / 105.0, -1.0 / 280.0)


def first_diff(padded, axis, count):
    summed = None
    for k in range(1, 5):
        upper_part = lax.slice_in_dim(padded, 4 + k, 4 + k + count, axis=axis)
        lower_part = lax.slice_in_dim(padded, 4 - k, 4 - k + count, axis=axis)
        addend = COEF[k - 1] * (upper_part - lower_part)
        summed = addend if summed is None else summed + addend
    return summed


def pad_axis(field, axis):
    widths = [(0, 0), (0, 0), (0, 0)]
    widths[axis] = (4, 4)
    return jnp.pad(field, widths)


def operate(field, tensor_parts):
    twice_eps, normal_x, normal_y, normal_z = tensor_parts
    slope_x = first_diff(pad_axis(field, 0), 0, field.shape[0])
    slope_y = first_diff(pad_axis(field, 1), 1, field.shape[1])
    slope_z = first_diff(pad_axis(field, 2), 2, field.shape[2])
    normal_slope = normal_x * slope_x + normal_y * slope_y + normal_z * slope_z
    flux_x = (1.0 + twice_eps) * slope_x - twice_eps * normal_x * normal_slope
    flux_y = (1.0 + twice_eps) * slope_y - twice_eps * normal_y * normal_slope
    flux_z = (1.0 + twice_eps) * slope_z - twice_eps * normal_z * normal_slope
    result = first_diff(pad_axis(flux_x, 0), 0, field.shape[0])
    result = result + first_diff(pad_axis(flux_y, 1), 1, field.shape[1])
    return result + first_diff(pad_axis(flux_z, 2), 2, field.shape[2])


def reference(state_before, state_now, adjoint_later, adjoint_now, courant_sq, epsilon, tilt_angle, azimuth, aperture_anchor, step_index, wavelet, residual_traces, source_x, source_y, source_z, receiver_x, receiver_y, receiver_z):
    start_step = step_index[0].astype(jnp.int32)

    def one_shot(grad_whole, shot_index):
        anchor = aperture_anchor[shot_index].astype(jnp.int32)

        def window(field):
            return lax.dynamic_slice_in_dim(field, anchor, NY, axis=1)

        speed_term = window(courant_sq)
        twice_eps = 2.0 * window(epsilon)
        tilt_part = window(tilt_angle)
        azimuth_part = window(azimuth)
        tensor_parts = (twice_eps, jnp.sin(tilt_part) * jnp.cos(azimuth_part), jnp.sin(tilt_part) * jnp.sin(azimuth_part), jnp.cos(tilt_part))
        previous = state_before[shot_index]
        current = state_now[shot_index]
        images = []
        for t in range(STEPS):
            image = operate(current, tensor_parts)
            images.append(image)
            if t < STEPS - 1:
                amplitude = lax.dynamic_index_in_dim(wavelet[shot_index], (start_step + t).astype(jnp.int32), keepdims=False)
                following = 2.0 * current - previous + speed_term * image
                following = following.at[source_x[shot_index], source_y[shot_index], source_z[shot_index]].add(amplitude)
                previous, current = current, following
        later = adjoint_later[shot_index]
        present = adjoint_now[shot_index]
        shot_grad = jnp.zeros((AX, NY, NZ), jnp.float32)
        for t in reversed(range(STEPS)):
            shot_grad = shot_grad + present * images[t]
            earlier = 2.0 * present - later + operate(speed_term * present, tensor_parts)
            samples = lax.dynamic_index_in_dim(residual_traces[shot_index], (start_step + t).astype(jnp.int32), keepdims=False)
            earlier = earlier.at[receiver_x[shot_index], receiver_y[shot_index], receiver_z[shot_index]].add(samples)
            later, present = present, earlier
        placed = lax.dynamic_slice_in_dim(grad_whole, anchor, NY, axis=1) + shot_grad
        zero_index = jnp.zeros((), jnp.int32)
        grad_whole = lax.dynamic_update_slice(grad_whole, placed, (zero_index, anchor, zero_index))
        return grad_whole, (later, present)

    grad_start = jnp.zeros((AX, NYG, NZ), jnp.float32)
    grad_whole, (adjoint_one, adjoint_zero) = lax.scan(one_shot, grad_start, jnp.arange(SHOTS, dtype=jnp.int32))
    return (adjoint_one, adjoint_zero, grad_whole)
```

```python
import functools

import jax
import jax.numpy as jnp
from jax import lax
from jax.experimental import pallas as pl
from jax.experimental.pallas import tpu as pltpu
from jax.sharding import PartitionSpec as P

STEPS = 4
COEF = (0.8, -0.2, 4.0 / 105.0, -1.0 / 280.0)
PAD = 8

VMEM = pl.BlockSpec(memory_space=pltpu.VMEM)
SMEM = pl.BlockSpec(memory_space=pltpu.SMEM)


def f32(*shape):
    return jax.ShapeDtypeStruct(shape, jnp.float32)


def call(body, outs, ins, scratch=(), cost=0):
    arrays = [a for a, _ in ins]
    return pl.pallas_call(
        body,
        out_shape=outs,
        in_specs=[s for _, s in ins],
        out_specs=jax.tree.map(lambda _: VMEM, outs),
        scratch_shapes=list(scratch),
        cost_estimate=pl.CostEstimate(flops=cost, bytes_accessed=1 << 20, transcendentals=0),
        compiler_params=pltpu.CompilerParams(vmem_limit_bytes=48 << 20),
    )(*arrays)


def depth_coefs(depth):
    lane = lax.broadcasted_iota(jnp.int32, (1, depth), 1)
    upper = [jnp.where(lane < depth - k, COEF[k - 1], 0.0) for k in range(1, 5)]
    lower = [jnp.where(lane >= k, COEF[k - 1], 0.0) for k in range(1, 5)]
    return upper, lower


def diff_z(tile, coefs):
    upper, lower = coefs
    depth = tile.shape[-1]
    summed = None
    for k in range(1, 5):
        term = upper[k - 1] * pltpu.roll(tile, depth - k, 1) - lower[k - 1] * pltpu.roll(tile, k, 1)
        summed = term if summed is None else summed + term
    return summed


def diff_rows(ref, row):
    summed = None
    for k in range(1, 5):
        term = COEF[k - 1] * (ref[row + k] - ref[row - k])
        summed = term if summed is None else summed + term
    return summed


def diff_y(ref, row, width):
    summed = None
    for k in range(1, 5):
        term = COEF[k - 1] * (
            ref[row, pl.ds(PAD + k, width), :] - ref[row, pl.ds(PAD - k, width), :]
        )
        summed = term if summed is None else summed + term
    return summed


def fill_field(own, partner, across, wide):
    rows, width, depth = own.shape
    odd = lax.axis_index("blk") % 2
    edge = jnp.zeros((3 * rows, PAD, depth), jnp.float32)
    wide[:, 0:PAD, :] = edge
    wide[:, PAD + width : 2 * PAD + width, :] = edge
    wide[rows : 2 * rows, PAD : PAD + width, :] = own[...]
    partner_at = jnp.where(odd == 1, 0, 2 * rows)
    across_at = jnp.where(odd == 1, 2 * rows, 0)
    wide[pl.ds(partner_at, rows), PAD : PAD + width, :] = partner[...]
    wide[pl.ds(across_at, rows), PAD : PAD + width, :] = across[...]


def apply_operator(wide, coef, flux_x, flux_y, part_z, finish):
    rows = part_z.shape[0]
    width, depth = part_z.shape[1], part_z.shape[2]
    coefs = depth_coefs(depth)
    edge = jnp.zeros((rows, PAD, depth), jnp.float32)
    flux_y[:, 0:PAD, :] = edge
    flux_y[:, PAD + width : 2 * PAD + width, :] = edge

    def slopes(i):
        slope_x = diff_rows_mid(wide, i + 4, width)
        slope_y = diff_y(wide, i + 4, width)
        slope_z = diff_z(wide[i + 4, PAD : PAD + width, :], coefs)
        along = coef[0, i] * slope_x + coef[1, i] * slope_y + coef[2, i] * slope_z
        flux_x[i] = coef[3, i] * slope_x - coef[0, i] * along
        return slope_y, slope_z, along

    def halo(i, _):
        slopes(i)
        slopes(i + rows + 4)
        return 0

    def inner(r, _):
        i = r + 4
        slope_y, slope_z, along = slopes(i)
        flux_y[r, PAD : PAD + width, :] = coef[3, i] * slope_y - coef[1, i] * along
        part_z[r] = diff_z(coef[3, i] * slope_z - coef[2, i] * along, coefs)
        return 0

    lax.fori_loop(0, 4, halo, 0)
    lax.fori_loop(0, rows, inner, 0)

    def last(r, _):
        finish(r, diff_rows(flux_x, r + 4) + diff_y(flux_y, r, width) + part_z[r])
        return 0

    lax.fori_loop(0, rows, last, 0)


def diff_rows_mid(ref, row, width):
    summed = None
    for k in range(1, 5):
        term = COEF[k - 1] * (
            ref[row + k, PAD : PAD + width, :] - ref[row - k, PAD : PAD + width, :]
        )
        summed = term if summed is None else summed + term
    return summed


def owner_kernel(speed, eps, tilt, azimuth, out):
    for r in range(speed.shape[0]):
        size = jnp.sqrt(2.0 * eps[r])
        flat = size * jnp.sin(tilt[r])
        out[0, r] = flat * jnp.cos(azimuth[r])
        out[1, r] = flat * jnp.sin(azimuth[r])
        out[2, r] = size * jnp.cos(tilt[r])
        out[3, r] = speed[r]


def prepare_kernel(step, sx, sy, sz, wavelet, rx, ry, rz, traces, src, inj):
    rows, width, depth = src.shape[1:]
    first = lax.axis_index("blk") * rows
    start = step[0]
    shape = (rows, width, depth)
    hit = (
        (lax.broadcasted_iota(jnp.int32, shape, 0) == sx[0] - first)
        & (lax.broadcasted_iota(jnp.int32, shape, 1) == sy[0])
        & (lax.broadcasted_iota(jnp.int32, shape, 2) == sz[0])
    )
    for t in range(STEPS - 1):
        src[t] = jnp.where(hit, wavelet[0, start + t], 0.0)
    receivers = rx.shape[1]
    local = rx[...] - first
    plane = jnp.where((local >= 0) & (local < rows), local * width + ry[...], -1)
    pick = (
        lax.broadcasted_iota(jnp.int32, (rows * width, receivers), 0) == plane
    ).astype(jnp.float32)
    match = lax.broadcasted_iota(jnp.int32, (depth, receivers), 0) == rz[...]
    for t in range(STEPS):
        samples = traces[0, pl.ds(start + t, 1), :]
        spread = jnp.where(match, samples, 0.0)
        added = lax.dot_general(
            pick,
            spread,
            (((1,), (1,)), ((), ())),
            precision=lax.Precision.HIGHEST,
            preferred_element_type=jnp.float32,
        )
        inj[t] = added.reshape(shape)


def window_kernel(shots, anchor, present, *refs):
    pieces = refs[:shots]
    tensor, speed, across, partner, operand = refs[shots:]
    rows, count, depth = pieces[0].shape[1:]
    parts = speed.shape[1] // count
    me = lax.axis_index("shot")
    first = anchor[0] // count
    for j in range(parts):
        place = slice(j * count, (j + 1) * count)
        slot = jnp.bitwise_xor(first + j, me)
        for k in range(shots):

            @pl.when(slot == k)
            def _():
                tensor[:, :, place, :] = pieces[k][0:3]
                speed[:, place, :] = pieces[k][3]

    odd = lax.axis_index("blk") % 2
    low = rows - 4
    across[...] = tensor[:, pl.ds(odd * low, 4)]
    partner[...] = tensor[:, pl.ds((1 - odd) * low, 4)]
    operand[...] = speed[...] * present[...]


def widen_coef(tensor, partner, across, coef):
    rows = tensor.shape[1]
    blk = lax.axis_index("blk")
    blocks = lax.axis_size("blk")
    odd = blk % 2
    coef[0:3, 4 : 4 + rows] = tensor[...]
    coef[0:3, pl.ds(jnp.where(odd == 1, 0, rows + 4), 4)] = partner[...]
    coef[0:3, pl.ds(jnp.where(odd == 1, rows + 4, 0), 4)] = across[...]
    for i in range(rows + 8):
        size = 1.0 + (coef[0, i] * coef[0, i] + coef[1, i] * coef[1, i] + coef[2, i] * coef[2, i])
        if i < 4:
            size = jnp.where(blk == 0, 0.0, size)
        if i >= rows + 4:
            size = jnp.where(blk == blocks - 1, 0.0, size)
        coef[3, i] = size


def forward_first(own, partner, across, tensor, tensor_p, tensor_a, previous, speed, src,
                  coef, image, following, wide, flux_x, flux_y, part_z):
    widen_coef(tensor, tensor_p, tensor_a, coef)
    forward(own, partner, across, coef, previous, speed, src, image, following,
            wide, flux_x, flux_y, part_z, t=0)


def forward(own, partner, across, coef, previous, speed, src, image, following,
            wide, flux_x, flux_y, part_z, t):
    fill_field(own, partner, across, wide)

    def finish(r, value):
        image[r] = value
        following[r] = 2.0 * own[r] - previous[r] + speed[r] * value + src[t, r]

    apply_operator(wide, coef, flux_x, flux_y, part_z, finish)


def backward(own, partner, across, coef, present, later, speed, inj, *rest, t):
    if t > 0:
        earlier, operand, wide, flux_x, flux_y, part_z = rest
    else:
        earlier, wide, flux_x, flux_y, part_z = rest
    fill_field(own, partner, across, wide)

    def finish(r, value):
        result = 2.0 * present[r] - later[r] + value + inj[t, r]
        earlier[r] = result
        if t > 0:
            operand[r] = speed[r] * result

    apply_operator(wide, coef, flux_x, flux_y, part_z, finish)


def forward_last(shots, anchor, own, partner, across, coef, *refs):
    adjoints = refs[:STEPS]
    images = refs[STEPS : 2 * STEPS - 1]
    out, wide, flux_x, flux_y, part_z, grad = refs[2 * STEPS - 1 :]
    count = out.shape[2]
    parts = grad.shape[1] // count
    fill_field(own, partner, across, wide)

    def finish(r, value):
        total = adjoints[STEPS - 1][r] * value
        for t in reversed(range(STEPS - 1)):
            total = total + adjoints[t][r] * images[t][r]
        grad[r] = total

    apply_operator(wide, coef, flux_x, flux_y, part_z, finish)
    me = lax.axis_index("shot")
    first = anchor[0] // count
    for k in range(shots):
        part = jnp.bitwise_xor(me, k) - first
        inside = (part >= 0) & (part < parts)
        at = pl.multiple_of(jnp.clip(part, 0, parts - 1) * count, 8)
        out[k] = jnp.where(inside, grad[:, pl.ds(at, count), :], 0.0)


def on_device(
    state_before,
    state_now,
    adjoint_later,
    adjoint_now,
    courant_sq,
    epsilon,
    tilt_angle,
    azimuth,
    aperture_anchor,
    step_index,
    wavelet,
    residual_traces,
    source_x,
    source_y,
    source_z,
    receiver_x,
    receiver_y,
    receiver_z,
):
    rows, width, depth = state_now.shape[1:]
    count = courant_sq.shape[1]
    shots = lax.axis_size("shot")
    blocks = lax.axis_size("blk")
    field = f32(rows, width, depth)
    core_pairs = [(i, i ^ 1) for i in range(blocks)]
    chip_pairs = [(i, i + 1) for i in range(1, blocks - 1, 2)]
    chip_pairs = chip_pairs + [(j, i) for i, j in chip_pairs]

    def halos(array):
        return (
            lax.ppermute(array, "blk", core_pairs),
            lax.ppermute(array, "blk", chip_pairs),
        )

    scratch = (
        pltpu.VMEM((3 * rows, width + 2 * PAD, depth), jnp.float32),
        pltpu.VMEM((rows + 8, width, depth), jnp.float32),
        pltpu.VMEM((rows, width + 2 * PAD, depth), jnp.float32),
        pltpu.VMEM((rows, width, depth), jnp.float32),
    )
    flops = 100 * (rows + 8) * width * depth

    own_piece = call(
        owner_kernel,
        f32(4, rows, count, depth),
        [(a, VMEM) for a in (courant_sq, epsilon, tilt_angle, azimuth)],
        cost=flops // 2,
    )
    pieces = [own_piece]
    for k in range(1, shots):
        pieces.append(lax.ppermute(own_piece, "shot", [(i, i ^ k) for i in range(shots)]))
    current = state_now[0]
    present = adjoint_now[0]
    now_p, now_a = halos(current)

    src, inj = call(
        prepare_kernel,
        (f32(STEPS - 1, rows, width, depth), f32(STEPS, rows, width, depth)),
        [(a, SMEM) for a in (step_index, source_x, source_y, source_z, wavelet)]
        + [(a, VMEM) for a in (receiver_x, receiver_y, receiver_z, residual_traces)],
        cost=flops,
    )
    edge = f32(3, 4, width, depth)
    tensor, speed, edge_a, edge_p, operand = call(
        functools.partial(window_kernel, shots),
        (f32(3, rows, width, depth), field, edge, edge, field),
        [(aperture_anchor, SMEM), (present, VMEM)] + [(a, VMEM) for a in pieces],
    )
    edge_a = lax.ppermute(edge_a, "blk", chip_pairs)
    edge_p = lax.ppermute(edge_p, "blk", core_pairs)
    op_p, op_a = halos(operand)

    coef, image, following = call(
        forward_first,
        (f32(4, rows + 8, width, depth), field, field),
        [
            (a, VMEM)
            for a in (current, now_p, now_a, tensor, edge_p, edge_a, state_before[0], speed, src)
        ],
        scratch,
        flops,
    )
    images = [image]
    previous, current = current, following
    adjoints = [present]
    later = adjoint_later[0]

    for t in range(STEPS - 1):
        now_p, now_a = halos(current)
        result = call(
            functools.partial(backward, t=STEPS - 1 - t),
            (field, field),
            [(a, VMEM) for a in (operand, op_p, op_a, coef, present, later, speed, inj)],
            scratch,
            flops,
        )
        later, present, operand = present, result[0], result[1]
        adjoints.append(present)
        op_p, op_a = halos(operand)
        if t < STEPS - 2:
            image, following = call(
                functools.partial(forward, t=t + 1),
                (field, field),
                [(a, VMEM) for a in (current, now_p, now_a, coef, previous, speed, src)],
                scratch,
                flops,
            )
            images.append(image)
            previous, current = current, following

    chunks = call(
        functools.partial(forward_last, shots),
        f32(shots, rows, count, depth),
        [(aperture_anchor, SMEM)]
        + [(a, VMEM) for a in (current, now_p, now_a, coef)]
        + [(a, VMEM) for a in adjoints[::-1]]
        + [(a, VMEM) for a in images],
        scratch + (pltpu.VMEM((rows, width, depth), jnp.float32),),
        flops,
    )
    received = [
        lax.ppermute(chunks[k], "shot", [(i, i ^ k) for i in range(shots)])
        for k in range(1, shots)
    ]
    (final,) = call(
        functools.partial(backward, t=0),
        (field,),
        [(a, VMEM) for a in (operand, op_p, op_a, coef, present, later, speed, inj)],
        scratch,
        flops,
    )
    model_grad = chunks[0]
    for piece in received:
        model_grad = model_grad + piece
    return (present[None], final[None], model_grad)


def solution(mesh):
    in_specs = (
        P("shot", "blk", None, None),
        P("shot", "blk", None, None),
        P("shot", "blk", None, None),
        P("shot", "blk", None, None),
        P("blk", "shot", None),
        P("blk", "shot", None),
        P("blk", "shot", None),
        P("blk", "shot", None),
        P("shot"),
        P(),
        P("shot", None),
        P("shot", None, None),
        P("shot"),
        P("shot"),
        P("shot"),
        P("shot", None),
        P("shot", None),
        P("shot", None),
    )
    out_specs = (P("shot", "blk", None, None), P("shot", "blk", None, None), P("blk", "shot", None))
    return jax.shard_map(
        on_device, mesh=mesh, in_specs=in_specs, out_specs=out_specs, check_vma=False
    )
```

```python
import functools

import jax
import jax.numpy as jnp
from jax import lax
from jax.experimental import pallas as pl
from jax.experimental.pallas import tpu as pltpu
from jax.sharding import PartitionSpec as P

STEPS = 4
COEF = (0.8, -0.2, 4.0 / 105.0, -1.0 / 280.0)
WHOLE = (672.0, -168.0, 32.0, -3.0)
UNIT = 1.0 / 840.0
PAD = 8

VMEM = pl.BlockSpec(memory_space=pltpu.VMEM)
SMEM = pl.BlockSpec(memory_space=pltpu.SMEM)
HBM = pl.BlockSpec(memory_space=pl.ANY)


def f32(*shape):
    return jax.ShapeDtypeStruct(shape, jnp.float32)


def call(name, body, outs, ins, scratch=(), flops=1 << 20):
    pairs = [a if isinstance(a, tuple) else (a, VMEM) for a in ins]
    return pl.pallas_call(
        body,
        name=name,
        out_shape=outs,
        in_specs=[s for _, s in pairs],
        out_specs=jax.tree.map(lambda _: VMEM, outs),
        scratch_shapes=list(scratch),
        cost_estimate=pl.CostEstimate(flops=flops, bytes_accessed=1 << 20, transcendentals=0),
        compiler_params=pltpu.CompilerParams(vmem_limit_bytes=48 << 20),
    )(*[a for a, _ in pairs])


def stencil(pick):
    summed = None
    for k in range(1, 5):
        term = COEF[k - 1] * (pick(k) - pick(-k))
        summed = term if summed is None else summed + term
    return summed


def diff_y(ref, row, width):
    return stencil(lambda k: ref[row, PAD + k : PAD + k + width, :])


def diff_z(tile, matrix):
    high = tile.astype(jnp.bfloat16)
    low = (tile - high.astype(jnp.float32)).astype(jnp.bfloat16)
    both = jnp.concatenate([high, low], axis=-1)
    return jnp.dot(both, matrix[...], preferred_element_type=jnp.float32) * UNIT


def place_halos(wide, lane, own, partner, across):
    rows, depth_rows = own.shape[0], partner.shape[0]
    blk, blocks = lax.axis_index("blk"), lax.axis_size("blk")
    odd = blk % 2
    outside = (blk == 0) | (blk == blocks - 1)
    above = depth_rows + rows
    wide[(slice(depth_rows, above), *lane)] = own[...]
    wide[(pl.ds(jnp.where(odd == 1, 0, above), depth_rows), *lane)] = partner[...]
    wide[(pl.ds(jnp.where(odd == 1, above, 0), depth_rows), *lane)] = jnp.where(
        outside, 0.0, across[...]
    )


def fill_field(own, partner, across, wide):
    rows, width, depth = own.shape
    edge = jnp.zeros((3 * rows, PAD, depth), jnp.float32)
    wide[:, 0:PAD, :] = edge
    wide[:, PAD + width : 2 * PAD + width, :] = edge
    place_halos(wide, (slice(PAD, PAD + width), slice(None)), own, partner, across)


def slopes_at(wide, i, width, matrix):
    inner = slice(PAD, PAD + width)
    return (
        stencil(lambda k: wide[i + k, inner, :]),
        diff_y(wide, i, width),
        diff_z(wide[i, inner, :], matrix),
    )


def clear_sides(flux_y, width):
    rows, _, depth = flux_y.shape
    edge = jnp.zeros((rows, PAD, depth), jnp.float32)
    flux_y[:, 0:PAD, :] = edge
    flux_y[:, PAD + width : 2 * PAD + width, :] = edge


def apply_operator(wide, coef, matrix, flux_x, flux_y, part_z, finish):
    rows, width, _ = part_z.shape
    clear_sides(flux_y, width)
    for i in range(rows + 8):
        slope_x, slope_y, slope_z = slopes_at(wide, i + 4, width, matrix)
        along = coef[0, i] * slope_x + coef[1, i] * slope_y + coef[2, i] * slope_z
        flux_x[i] = coef[3, i] * slope_x - coef[0, i] * along
        r = i - 4
        if 0 <= r < rows:
            flux_y[r, PAD : PAD + width, :] = coef[3, i] * slope_y - coef[1, i] * along
            part_z[r] = diff_z(coef[3, i] * slope_z - coef[2, i] * along, matrix)
    for r in range(rows):
        finish(r, stencil(lambda k: flux_x[r + 4 + k]) + diff_y(flux_y, r, width) + part_z[r])


def owner_kernel(eps, tilt, azimuth, out, held, sems):
    copies = [
        pltpu.make_async_copy(ref, held.at[n], sems.at[n])
        for n, ref in enumerate((eps, tilt, azimuth))
    ]
    for copy in copies:
        copy.start()
    for copy in copies:
        copy.wait()
    for r in range(out.shape[1]):
        size = jnp.sqrt(2.0 * held[0, r])
        flat = size * jnp.sin(held[1, r])
        out[0, r] = flat * jnp.cos(held[2, r])
        out[1, r] = flat * jnp.sin(held[2, r])
        out[2, r] = size * jnp.cos(held[1, r])


def prepare_kernel(shots, parts, step, anchor, sx, sy, sz, wavelet, rx, ry, rz, traces, speed,
                   own, partner, across, slope, src, inj, flags, matrix, speed_out, wide):
    rows, width, depth = src.shape[1:]
    count = speed.shape[1]
    speed_out[...] = speed[...]
    shape = matrix.shape
    offset = lax.broadcasted_iota(jnp.int32, shape, 0) % depth - lax.broadcasted_iota(
        jnp.int32, shape, 1
    )
    entries = jnp.zeros(shape, jnp.float32)
    for k in range(1, 5):
        entries = jnp.where(offset == k, WHOLE[k - 1], entries)
        entries = jnp.where(offset == -k, -WHOLE[k - 1], entries)
    matrix[...] = entries.astype(jnp.bfloat16)
    fill_field(own, partner, across, wide)
    for r in range(rows):
        slope[0, r], slope[1, r], slope[2, r] = slopes_at(wide, rows + r, width, matrix)
    me = lax.axis_index("shot")
    first_part = anchor[0] // count
    for k in range(shots):
        part = jnp.bitwise_xor(me, k) - first_part
        for j in range(parts):
            flags[k * parts + j : k * parts + j + 1, :] = jnp.full(
                (1, depth), jnp.where(part == j, 1.0, 0.0), jnp.float32
            )
    first = lax.axis_index("blk") * rows
    start = step[0]
    shape = (rows, width, depth)
    hit = (
        (lax.broadcasted_iota(jnp.int32, shape, 0) == sx[0] - first)
        & (lax.broadcasted_iota(jnp.int32, shape, 1) == sy[0])
        & (lax.broadcasted_iota(jnp.int32, shape, 2) == sz[0])
    )
    for t in range(STEPS - 1):
        src[t] = jnp.where(hit, wavelet[0, start + t], 0.0)
    receivers = rx.shape[1]
    local = rx[...] - first
    plane = jnp.where((local >= 0) & (local < rows), local * width + ry[...], -1)
    pick = (
        lax.broadcasted_iota(jnp.int32, (rows * width, receivers), 0) == plane
    ).astype(jnp.float32)
    match = lax.broadcasted_iota(jnp.int32, (depth, receivers), 0) == rz[...]
    for t in range(STEPS):
        samples = traces[0, pl.ds(start + t, 1), :]
        spread = jnp.where(match, samples, 0.0)
        added = lax.dot_general(
            pick,
            spread,
            (((1,), (1,)), ((), ())),
            precision=lax.Precision.HIGHEST,
            preferred_element_type=jnp.float32,
        )
        inj[t] = added.reshape(shape)


def window_part(pieces, flags, parts, j):
    chosen = pieces[-1][...]
    for k in reversed(range(len(pieces) - 1)):
        at = k * parts + j
        chosen = jnp.where(flags[at : at + 1, :] > 0.5, pieces[k][...], chosen)
    return chosen


def flux_kernel(shots, parts, *refs):
    pieces = refs[:shots]
    (flags, slope, matrix, tensor, flux, rest, flux_a, flux_p, edge_a, edge_p, flux_y) = refs[
        shots:
    ]
    rows, width, _ = flux.shape
    count = width // parts
    for j in range(parts):
        tensor[:, :, j * count : (j + 1) * count, :] = window_part(pieces, flags, parts, j)
    clear_sides(flux_y, width)
    for r in range(rows):
        wx, wy, wz = tensor[0, r], tensor[1, r], tensor[2, r]
        along = wx * slope[0, r] + wy * slope[1, r] + wz * slope[2, r]
        size = 1.0 + (wx * wx + wy * wy + wz * wz)
        flux[r] = size * slope[0, r] - wx * along
        flux_y[r, PAD : PAD + width, :] = size * slope[1, r] - wy * along
        rest[r] = diff_z(size * slope[2, r] - wz * along, matrix)
    for r in range(rows):
        rest[r] = rest[r] + diff_y(flux_y, r, width)
    odd = lax.axis_index("blk") % 2
    low = rows - 4
    flux_a[...] = flux[pl.ds(odd * low, 4)]
    flux_p[...] = flux[pl.ds((1 - odd) * low, 4)]
    edge_a[...] = tensor[:, pl.ds(odd * low, 4)]
    edge_p[...] = tensor[:, pl.ds((1 - odd) * low, 4)]


def speed_kernel(shots, parts, *refs):
    pieces = refs[:shots]
    flags, present, speed, operand = refs[shots:]
    count = speed.shape[1] // parts
    for j in range(parts):
        speed[:, j * count : (j + 1) * count, :] = window_part(pieces, flags, parts, j)
    operand[...] = speed[...] * present[...]


def coef_kernel(tensor, partner, across, coef):
    rows = tensor.shape[1]
    blk, blocks = lax.axis_index("blk"), lax.axis_size("blk")
    for a in range(3):
        place_halos(coef.at[a], (), tensor.at[a], partner.at[a], across.at[a])
    for i in range(rows + 8):
        size = 1.0 + (coef[0, i] * coef[0, i] + coef[1, i] * coef[1, i] + coef[2, i] * coef[2, i])
        if i < 4:
            size = jnp.where(blk == 0, 0.0, size)
        if i >= rows + 4:
            size = jnp.where(blk == blocks - 1, 0.0, size)
        coef[3, i] = size


def forward_first(flux, flux_p, flux_a, rest, own, previous, speed, src, image, following, flux_x):
    place_halos(flux_x, (), flux, flux_p, flux_a)
    for r in range(rest.shape[0]):
        value = stencil(lambda k: flux_x[r + 4 + k]) + rest[r]
        image[r] = value
        following[r] = 2.0 * own[r] - previous[r] + speed[r] * value + src[0, r]


def forward(t, own, partner, across, coef, matrix, previous, speed, src, image, following,
            wide, *scratch):
    fill_field(own, partner, across, wide)

    def finish(r, value):
        image[r] = value
        following[r] = 2.0 * own[r] - previous[r] + speed[r] * value + src[t, r]

    apply_operator(wide, coef, matrix, *scratch, finish)


def backward(t, own, partner, across, coef, matrix, present, later, inj, *refs):
    if t == 0:
        (earlier,) = refs[:1]
    elif t == 1:
        speed, lambda3, image0, image1, image2, earlier, operand, known = refs[:8]
    else:
        speed, earlier, operand = refs[:3]
    wide, flux_x, flux_y, part_z = refs[-4:]
    fill_field(own, partner, across, wide)

    def finish(r, value):
        result = 2.0 * present[r] - later[r] + value + inj[t, r]
        earlier[r] = result
        if t > 0:
            operand[r] = speed[r] * result
        if t == 1:
            known[r] = lambda3[r] * image2[r] + present[r] * image1[r] + result * image0[r]

    apply_operator(wide, coef, matrix, flux_x, flux_y, part_z, finish)


def forward_last(parts, own, partner, across, coef, matrix, known, lambda4, flags, *refs):
    *chunks, wide, flux_x, flux_y, part_z, grad = refs
    count = chunks[0].shape[1]
    fill_field(own, partner, across, wide)

    def finish(r, value):
        grad[r] = known[r] + lambda4[r] * value

    apply_operator(wide, coef, matrix, flux_x, flux_y, part_z, finish)
    for k, chunk in enumerate(chunks):
        held = jnp.zeros(chunk.shape, jnp.float32)
        for j in range(parts):
            at = k * parts + j
            held = jnp.where(
                flags[at : at + 1, :] > 0.5, grad[:, j * count : (j + 1) * count, :], held
            )
        chunk[...] = held


def on_device(
    state_before,
    state_now,
    adjoint_later,
    adjoint_now,
    courant_sq,
    epsilon,
    tilt_angle,
    azimuth,
    aperture_anchor,
    step_index,
    wavelet,
    residual_traces,
    source_x,
    source_y,
    source_z,
    receiver_x,
    receiver_y,
    receiver_z,
):
    rows, width, depth = state_now.shape[1:]
    count = courant_sq.shape[1]
    parts = width // count
    shots = lax.axis_size("shot")
    blocks = lax.axis_size("blk")
    field = f32(rows, width, depth)
    wide = (rows, width + 2 * PAD, depth)
    scratch = (
        pltpu.VMEM((3 * rows, width + 2 * PAD, depth), jnp.float32),
        pltpu.VMEM((rows + 8, width, depth), jnp.float32),
        pltpu.VMEM(wide, jnp.float32),
        pltpu.VMEM((rows, width, depth), jnp.float32),
    )
    work = 100 * (rows + 8) * width * depth

    core_pairs = [(i, i ^ 1) for i in range(blocks)]
    chip_pairs = []
    for s in range(shots):
        for b in range(blocks):
            end = b in (0, blocks - 1)
            other = (s ^ 1, b) if end else (s, b - 1 + 2 * (b % 2))
            chip_pairs.append((s * blocks + b, other[0] * blocks + other[1]))

    def to_partner(array):
        return lax.ppermute(array, "blk", core_pairs)

    def across_chips(array):
        return lax.ppermute(array, ("shot", "blk"), chip_pairs)

    def to_owners(array, k):
        return lax.ppermute(array, "shot", [(i, i ^ k) for i in range(shots)])

    current, previous = state_now[0], state_before[0]
    present, later = adjoint_now[0], adjoint_later[0]

    piece = call(
        "owner",
        owner_kernel,
        f32(3, rows, count, depth),
        [(a, HBM) for a in (epsilon, tilt_angle, azimuth)],
        (pltpu.VMEM((3, rows, count, depth), jnp.float32), pltpu.SemaphoreType.DMA((3,))),
    )
    pieces = [piece] + [to_owners(piece, k) for k in range(1, shots)]
    now_a = across_chips(current)
    now_p = to_partner(current)

    slope, src, inj, flags, matrix, speed_piece = call(
        "prepare",
        functools.partial(prepare_kernel, shots, parts),
        (
            f32(3, rows, width, depth),
            f32(STEPS - 1, rows, width, depth),
            f32(STEPS, rows, width, depth),
            f32(shots * parts, depth),
            jax.ShapeDtypeStruct((2 * depth, depth), jnp.bfloat16),
            f32(rows, count, depth),
        ),
        [
            (a, SMEM)
            for a in (step_index, aperture_anchor, source_x, source_y, source_z, wavelet)
        ]
        + [receiver_x, receiver_y, receiver_z, residual_traces, courant_sq]
        + [current, now_p, now_a],
        scratch[:1],
        work,
    )
    speed_pieces = [speed_piece] + [to_owners(speed_piece, k) for k in range(1, shots)]

    flux_edge, edge = f32(4, width, depth), f32(3, 4, width, depth)
    tensor, flux, rest, flux_a, flux_p, edge_a, edge_p = call(
        "flux",
        functools.partial(flux_kernel, shots, parts),
        (f32(3, rows, width, depth), field, field, flux_edge, flux_edge, edge, edge),
        pieces + [flags, slope, matrix],
        scratch[2:3],
        work // 3,
    )
    flux_a = across_chips(flux_a)
    flux_p = to_partner(flux_p)
    edge_a = across_chips(edge_a)
    edge_p = to_partner(edge_p)

    speed, operand = call(
        "speed",
        functools.partial(speed_kernel, shots, parts),
        (field, field),
        speed_pieces + [flags, present],
    )
    op_a = across_chips(operand)
    op_p = to_partner(operand)

    image, following = call(
        "forward0",
        forward_first,
        (field, field),
        [flux, flux_p, flux_a, rest, current, previous, speed, src],
        scratch[1:2],
        work // 4,
    )
    coef = call("coef", coef_kernel, f32(4, rows + 8, width, depth), [tensor, edge_p, edge_a])
    images = [image]
    previous, current = current, following
    adjoints = [present]
    known = None
    for t in range(STEPS - 1):
        now_a = across_chips(current)
        now_p = to_partner(current)
        back = STEPS - 1 - t
        ins = [operand, op_p, op_a, coef, matrix, present, later, inj, speed]
        outs = (field, field)
        if back == 1:
            ins = ins + [adjoints[1]] + images
            outs = (field, field, field)
        result = call(
            f"backward{t}", functools.partial(backward, back), outs, ins, scratch, work
        )
        later, present, operand = present, result[0], result[1]
        if back == 1:
            known = result[2]
        adjoints.append(present)
        op_a = across_chips(operand)
        op_p = to_partner(operand)
        if t < STEPS - 2:
            image, following = call(
                f"forward{t + 1}",
                functools.partial(forward, t + 1),
                (field, field),
                [current, now_p, now_a, coef, matrix, previous, speed, src],
                scratch,
                work,
            )
            images.append(image)
            previous, current = current, following

    chunks = call(
        "forward3",
        functools.partial(forward_last, parts),
        (f32(rows, count, depth),) * shots,
        [current, now_p, now_a, coef, matrix, known, adjoints[0], flags],
        scratch + (pltpu.VMEM((rows, width, depth), jnp.float32),),
        work,
    )
    received = [to_owners(chunks[k], k) for k in range(1, shots)]
    (final,) = call(
        "backward3",
        functools.partial(backward, 0),
        (field,),
        [operand, op_p, op_a, coef, matrix, present, later, inj],
        scratch,
        work,
    )
    model_grad = chunks[0]
    for part in received:
        model_grad = model_grad + part
    return (present[None], final[None], model_grad)


def solution(mesh):
    in_specs = (
        P("shot", "blk", None, None),
        P("shot", "blk", None, None),
        P("shot", "blk", None, None),
        P("shot", "blk", None, None),
        P("blk", "shot", None),
        P("blk", "shot", None),
        P("blk", "shot", None),
        P("blk", "shot", None),
        P("shot"),
        P(),
        P("shot", None),
        P("shot", None, None),
        P("shot"),
        P("shot"),
        P("shot"),
        P("shot", None),
        P("shot", None),
        P("shot", None),
    )
    out_specs = (P("shot", "blk", None, None), P("shot", "blk", None, None), P("blk", "shot", None))
    return jax.shard_map(
        on_device, mesh=mesh, in_specs=in_specs, out_specs=out_specs, check_vma=False
    )
```

```python
import functools

import jax
import jax.numpy as jnp
from jax import lax
from jax.experimental import pallas as pl
from jax.experimental.pallas import tpu as pltpu
from jax.sharding import PartitionSpec as P

STEPS = 4
COEF = (0.8, -0.2, 4.0 / 105.0, -1.0 / 280.0)
WHOLE = (672.0, -168.0, 32.0, -3.0)
UNIT = 1.0 / 840.0
PAD = 8

VMEM = pl.BlockSpec(memory_space=pltpu.VMEM)
SMEM = pl.BlockSpec(memory_space=pltpu.SMEM)
HBM = pl.BlockSpec(memory_space=pltpu.HBM)


def f32(*shape):
    return jax.ShapeDtypeStruct(shape, jnp.float32)


def call(name, body, outs, ins, scratch=(), flops=1 << 20):
    pairs = [a if isinstance(a, tuple) else (a, VMEM) for a in ins]
    return pl.pallas_call(
        body,
        name=name,
        out_shape=outs,
        in_specs=[s for _, s in pairs],
        out_specs=jax.tree.map(lambda _: VMEM, outs),
        scratch_shapes=list(scratch),
        cost_estimate=pl.CostEstimate(flops=flops, bytes_accessed=1 << 20, transcendentals=0),
        compiler_params=pltpu.CompilerParams(vmem_limit_bytes=48 << 20),
    )(*[a for a, _ in pairs])


def stencil(pick):
    summed = None
    for k in range(1, 5):
        term = COEF[k - 1] * (pick(k) - pick(-k))
        summed = term if summed is None else summed + term
    return summed


def diff_y(ref, row, width):
    return stencil(lambda k: ref[row, PAD + k : PAD + k + width, :])


def diff_z(tile, matrix):
    high = tile.astype(jnp.bfloat16)
    low = (tile - high.astype(jnp.float32)).astype(jnp.bfloat16)
    both = jnp.concatenate([high, low], axis=-1)
    return jnp.dot(both, matrix[...], preferred_element_type=jnp.float32) * UNIT


def place_halos(wide, lane, own, partner, across):
    rows, depth_rows = own.shape[0], partner.shape[0]
    blk, blocks = lax.axis_index("blk"), lax.axis_size("blk")
    odd = blk % 2
    outside = (blk == 0) | (blk == blocks - 1)
    above = depth_rows + rows
    wide[(slice(depth_rows, above), *lane)] = own[...]
    wide[(pl.ds(jnp.where(odd == 1, 0, above), depth_rows), *lane)] = partner[...]
    wide[(pl.ds(jnp.where(odd == 1, above, 0), depth_rows), *lane)] = jnp.where(
        outside, 0.0, across[...]
    )


def fill_field(own, partner, across, wide):
    rows, width, depth = own.shape
    edge = jnp.zeros((3 * rows, PAD, depth), jnp.float32)
    wide[:, 0:PAD, :] = edge
    wide[:, PAD + width : 2 * PAD + width, :] = edge
    place_halos(wide, (slice(PAD, PAD + width), slice(None)), own, partner, across)


def slopes_at(wide, i, width, matrix):
    inner = slice(PAD, PAD + width)
    return (
        stencil(lambda k: wide[i + k, inner, :]),
        diff_y(wide, i, width),
        diff_z(wide[i, inner, :], matrix),
    )


def clear_sides(flux_y, width):
    rows, _, depth = flux_y.shape
    edge = jnp.zeros((rows, PAD, depth), jnp.float32)
    flux_y[:, 0:PAD, :] = edge
    flux_y[:, PAD + width : 2 * PAD + width, :] = edge


def apply_operator(wide, coef, matrix, flux_x, flux_y, part_z, finish):
    rows, width, _ = part_z.shape
    clear_sides(flux_y, width)
    for i in range(rows + 8):
        slope_x, slope_y, slope_z = slopes_at(wide, i + 4, width, matrix)
        along = coef[0, i] * slope_x + coef[1, i] * slope_y + coef[2, i] * slope_z
        flux_x[i] = coef[3, i] * slope_x - coef[0, i] * along
        r = i - 4
        if 0 <= r < rows:
            flux_y[r, PAD : PAD + width, :] = coef[3, i] * slope_y - coef[1, i] * along
            part_z[r] = diff_z(coef[3, i] * slope_z - coef[2, i] * along, matrix)
    for r in range(rows):
        finish(r, stencil(lambda k: flux_x[r + 4 + k]) + diff_y(flux_y, r, width) + part_z[r])


def sin_cos(angle):
    square = angle * angle
    sine, cosine = 0.0, 1.0 / 479001600.0
    for factor in (-39916800.0, 362880.0, -5040.0, 120.0, -6.0, 1.0):
        sine = sine * square + 1.0 / factor
    for factor in (-3628800.0, 40320.0, -720.0, 24.0, -2.0, 1.0):
        cosine = cosine * square + 1.0 / factor
    return angle * sine, cosine


def owner_kernel(eps, tilt, azimuth, anchor, wx, wy, wz, first, held, held_anchor, sems):
    rows, count, _ = wx.shape
    copies = [
        pltpu.make_async_copy(ref, held.at[n], sems.at[n])
        for n, ref in enumerate((eps, tilt, azimuth))
    ]
    copies.append(pltpu.make_async_copy(anchor, held_anchor, sems.at[3]))
    for copy in copies:
        copy.start()
    for copy in copies:
        copy.wait()
    for r in range(rows):
        size = jnp.sqrt(2.0 * held[0, r])
        sin_tilt, cos_tilt = sin_cos(held[1, r])
        sin_half, cos_half = sin_cos(0.5 * held[2, r])
        flat = size * sin_tilt
        wx[r] = flat * (1.0 - 2.0 * sin_half * sin_half)
        wy[r] = flat * (2.0 * sin_half * cos_half)
        wz[r] = size * cos_tilt
    first[...] = jnp.full(first.shape, (held_anchor[0] // count).astype(jnp.float32))


def prepare_kernel(shots, parts, step, anchor, sx, sy, sz, wavelet, rx, ry, rz, traces,
                   own, partner, across, slope, src, inj, flags, matrix,
                   wide, scalars, wave, receiver, samples_held, sems):
    rows, width, depth = src.shape[1:]
    copies = [
        pltpu.make_async_copy(ref, scalars[n], sems.at[n])
        for n, ref in enumerate((step, anchor, sx, sy, sz))
    ]
    copies.append(pltpu.make_async_copy(wavelet, wave, sems.at[5]))
    for n, ref in enumerate((rx, ry, rz)):
        copies.append(pltpu.make_async_copy(ref, receiver[n], sems.at[6 + n]))
    copies.append(pltpu.make_async_copy(traces, samples_held, sems.at[9]))
    for copy in copies:
        copy.start()
    shape = matrix.shape
    offset = lax.broadcasted_iota(jnp.int32, shape, 0) % depth - lax.broadcasted_iota(
        jnp.int32, shape, 1
    )
    entries = jnp.zeros(shape, jnp.float32)
    for k in range(1, 5):
        entries = jnp.where(offset == k, WHOLE[k - 1], entries)
        entries = jnp.where(offset == -k, -WHOLE[k - 1], entries)
    matrix[...] = entries.astype(jnp.bfloat16)
    fill_field(own, partner, across, wide)
    for i in range(rows + 8):
        slope[0, i], slope[1, i], slope[2, i] = slopes_at(wide, i + 4, width, matrix)
    for copy in copies:
        copy.wait()
    me = lax.axis_index("shot")
    first_part = scalars[1][0] // (width // parts)
    for k in range(shots):
        part = jnp.bitwise_xor(me, k) - first_part
        for j in range(parts):
            flags[k * parts + j : k * parts + j + 1, :] = jnp.full(
                (1, depth), jnp.where(part == j, 1.0, 0.0), jnp.float32
            )
    first = lax.axis_index("blk") * rows
    start = scalars[0][0]
    shape = (rows, width, depth)
    hit = (
        (lax.broadcasted_iota(jnp.int32, shape, 0) == scalars[2][0] - first)
        & (lax.broadcasted_iota(jnp.int32, shape, 1) == scalars[3][0])
        & (lax.broadcasted_iota(jnp.int32, shape, 2) == scalars[4][0])
    )
    moment = lax.broadcasted_iota(jnp.int32, wave.shape, 1)
    for t in range(STEPS - 1):
        value = jnp.sum(jnp.where(moment == start + t, wave[...], 0.0), axis=1, keepdims=True)
        src[t] = jnp.where(hit, value, 0.0)
    receivers = rx.shape[1]
    local = receiver[0][...] - first
    plane = jnp.where((local >= 0) & (local < rows), local * width + receiver[1][...], -1)
    pick = (
        lax.broadcasted_iota(jnp.int32, (rows * width, receivers), 0) == plane
    ).astype(jnp.float32)
    match = lax.broadcasted_iota(jnp.int32, (depth, receivers), 0) == receiver[2][...]
    for t in range(STEPS):
        samples = samples_held[0, pl.ds(start + t, 1), :]
        spread = jnp.where(match, samples, 0.0)
        added = lax.dot_general(
            pick,
            spread,
            (((1,), (1,)), ((), ())),
            precision=lax.Precision.HIGHEST,
            preferred_element_type=jnp.float32,
        )
        inj[t] = added.reshape(shape)


def relay_kernel(parts, first, own, received, *refs):
    out = refs[-1] if len(refs) < 3 else refs[-2]
    part = lax.axis_index("shot").astype(jnp.float32) - first[0:1, :]
    inside = (part > -0.5) & (part < parts - 0.5)
    out[...] = jnp.where(inside, own[...], received[...])
    if len(refs) >= 3:
        refs[-1][...] = refs[0][...]


def window_part(pieces, flags, parts, j):
    chosen = pieces[-1][...]
    for k in reversed(range(len(pieces) - 1)):
        at = k * parts + j
        chosen = jnp.where(flags[at : at + 1, :] > 0.5, pieces[k][...], chosen)
    return chosen


def edge_rows(field, out_a, out_p):
    odd = lax.axis_index("blk") % 2
    low = field.shape[0] - 4
    out_a[...] = field[pl.ds(odd * low, 4)]
    out_p[...] = field[pl.ds((1 - odd) * low, 4)]


def window_kernel(slots, parts, *refs):
    held = max(slots) + 1
    flags, tensor, edge_a, edge_p = refs[2 * held :]
    count = tensor.shape[2] // parts
    for a in range(2):
        pieces = [refs[a * held + slot] for slot in slots]
        for j in range(parts):
            tensor[a, :, j * count : (j + 1) * count, :] = window_part(pieces, flags, parts, j)
        edge_rows(tensor.at[a], edge_a.at[a], edge_p.at[a])


def flux_kernel(slots, parts, *refs):
    held = max(slots) + 1
    pieces = [refs[slot] for slot in slots]
    flags, tensor, slope, matrix, _, last, flux, rest, edge_a, edge_p, flux_y = refs[held:]
    rows, width, _ = flux.shape
    count = width // parts
    for j in range(parts):
        last[:, j * count : (j + 1) * count, :] = window_part(pieces, flags, parts, j)
    edge_rows(last, edge_a, edge_p)
    clear_sides(flux_y, width)
    for r in range(rows):
        wx, wy, wz = tensor[0, r], tensor[1, r], last[r]
        along = wx * slope[0, r + 4] + wy * slope[1, r + 4] + wz * slope[2, r + 4]
        size = 1.0 + (wx * wx + wy * wy + wz * wz)
        flux[r] = size * slope[0, r + 4] - wx * along
        flux_y[r, PAD : PAD + width, :] = size * slope[1, r + 4] - wy * along
        rest[r] = diff_z(size * slope[2, r + 4] - wz * along, matrix)
    for r in range(rows):
        rest[r] = rest[r] + diff_y(flux_y, r, width)


def speed_kernel(slots, parts, *refs):
    held = max(slots) + 1
    pieces = [refs[slot] for slot in slots]
    flags, present, speed, operand = refs[held:]
    count = speed.shape[1] // parts
    for j in range(parts):
        speed[:, j * count : (j + 1) * count, :] = window_part(pieces, flags, parts, j)
    operand[...] = speed[...] * present[...]


def forward_first(tensor, tensor_p, tensor_a, last, last_p, last_a, slope, flux, rest,
                  own, previous, speed, src, image, following, coef, flux_x):
    rows = rest.shape[0]
    blk, blocks = lax.axis_index("blk"), lax.axis_size("blk")
    for a in range(2):
        place_halos(coef.at[a], (), tensor.at[a], tensor_p.at[a], tensor_a.at[a])
    place_halos(coef.at[2], (), last, last_p, last_a)
    for i in range(rows + 8):
        wx, wy, wz = coef[0, i], coef[1, i], coef[2, i]
        size = 1.0 + (wx * wx + wy * wy + wz * wz)
        if i < 4:
            size = jnp.where(blk == 0, 0.0, size)
        if i >= rows + 4:
            size = jnp.where(blk == blocks - 1, 0.0, size)
        coef[3, i] = size
        if 4 <= i < rows + 4:
            flux_x[i] = flux[i - 4]
        else:
            along = wx * slope[0, i] + wy * slope[1, i] + wz * slope[2, i]
            flux_x[i] = size * slope[0, i] - wx * along
    for r in range(rows):
        value = stencil(lambda k: flux_x[r + 4 + k]) + rest[r]
        image[r] = value
        following[r] = 2.0 * own[r] - previous[r] + speed[r] * value + src[0, r]


def forward(t, own, partner, across, coef, matrix, previous, speed, src, image, following,
            wide, *scratch):
    fill_field(own, partner, across, wide)

    def finish(r, value):
        image[r] = value
        following[r] = 2.0 * own[r] - previous[r] + speed[r] * value + src[t, r]

    apply_operator(wide, coef, matrix, *scratch, finish)


def backward(t, own, partner, across, coef, matrix, present, later, inj, *refs):
    if t == 0:
        earlier, copied = refs[:2]
        copied[...] = present[...]
    elif t == 1:
        speed, lambda3, image0, image1, image2, earlier, operand, known = refs[:8]
    else:
        speed, earlier, operand = refs[:3]
    wide, flux_x, flux_y, part_z = refs[-4:]
    fill_field(own, partner, across, wide)

    def finish(r, value):
        result = 2.0 * present[r] - later[r] + value + inj[t, r]
        earlier[r] = result
        if t > 0:
            operand[r] = speed[r] * result
        if t == 1:
            known[r] = lambda3[r] * image2[r] + present[r] * image1[r] + result * image0[r]

    apply_operator(wide, coef, matrix, flux_x, flux_y, part_z, finish)


def forward_last(parts, own, partner, across, coef, matrix, known, lambda4, flags, *refs):
    *chunks, wide, flux_x, flux_y, part_z, grad = refs
    count = chunks[0].shape[1]
    fill_field(own, partner, across, wide)

    def finish(r, value):
        grad[r] = known[r] + lambda4[r] * value

    apply_operator(wide, coef, matrix, flux_x, flux_y, part_z, finish)
    for k, chunk in enumerate(chunks):
        held = jnp.zeros(chunk.shape, jnp.float32)
        for j in range(parts):
            at = k * parts + j
            held = jnp.where(
                flags[at : at + 1, :] > 0.5, grad[:, j * count : (j + 1) * count, :], held
            )
        chunk[...] = held


def total_kernel(*refs):
    out = refs[-1]
    total = refs[0][...]
    for ref in refs[1:-2]:
        total = total + ref[...]
    out[...] = total


def on_device(
    state_before,
    state_now,
    adjoint_later,
    adjoint_now,
    courant_sq,
    epsilon,
    tilt_angle,
    azimuth,
    aperture_anchor,
    step_index,
    wavelet,
    residual_traces,
    source_x,
    source_y,
    source_z,
    receiver_x,
    receiver_y,
    receiver_z,
):
    rows, width, depth = state_now.shape[1:]
    count = courant_sq.shape[1]
    parts = width // count
    shots = lax.axis_size("shot")
    blocks = lax.axis_size("blk")
    field = f32(rows, width, depth)
    wide = (rows, width + 2 * PAD, depth)
    scratch = (
        pltpu.VMEM((3 * rows, width + 2 * PAD, depth), jnp.float32),
        pltpu.VMEM((rows + 8, width, depth), jnp.float32),
        pltpu.VMEM(wide, jnp.float32),
        pltpu.VMEM((rows, width, depth), jnp.float32),
    )
    work = 100 * (rows + 8) * width * depth

    core_pairs = [(i, i ^ 1) for i in range(blocks)]
    chip_pairs = []
    for s in range(shots):
        for b in range(blocks):
            end = b in (0, blocks - 1)
            other = (s ^ 1, b) if end else (s, b - 1 + 2 * (b % 2))
            chip_pairs.append((s * blocks + b, other[0] * blocks + other[1]))

    def to_partner(array):
        return lax.ppermute(array, "blk", core_pairs)

    def across_chips(array):
        return lax.ppermute(array, ("shot", "blk"), chip_pairs)

    def to_owners(array, k):
        return lax.ppermute(array, "shot", [(i, i ^ k) for i in range(shots)])

    current, previous = state_now[0], state_before[0]
    present, later = adjoint_now[0], adjoint_later[0]

    wx, wy, wz, first = call(
        "owner",
        owner_kernel,
        (f32(rows, count, depth),) * 3 + (f32(8, depth),),
        [(a, HBM) for a in (epsilon, tilt_angle, azimuth, aperture_anchor)],
        (
            pltpu.VMEM((3, rows, count, depth), jnp.float32),
            pltpu.SMEM((1,), jnp.int32),
            pltpu.SemaphoreType.DMA((4,)),
        ),
    )
    model = [wx, wy, wz, courant_sq]
    piece = f32(rows, count, depth)

    def prepare():
        now_a = across_chips(current)
        now_p = to_partner(current)
        return call(
            "prepare",
            functools.partial(prepare_kernel, shots, parts),
            (
                f32(3, rows + 8, width, depth),
                f32(STEPS - 1, rows, width, depth),
                f32(STEPS, rows, width, depth),
                f32(shots * parts, depth),
                jax.ShapeDtypeStruct((2 * depth, depth), jnp.bfloat16),
            ),
            [
                (a, HBM)
                for a in (step_index, aperture_anchor, source_x, source_y, source_z, wavelet)
                + (receiver_x, receiver_y, receiver_z, residual_traces)
            ]
            + [current, now_p, now_a],
            (
                scratch[0],
                [pltpu.SMEM((1,), jnp.int32)] * 5,
                pltpu.VMEM(wavelet.shape, jnp.float32),
                [pltpu.VMEM(receiver_x.shape, jnp.int32)] * 3,
                pltpu.VMEM(residual_traces.shape, jnp.float32),
                pltpu.SemaphoreType.DMA((10,)),
            ),
            work,
        )

    if shots == 4 and parts == 2:
        slots = (0, 1, 2, 1)
        relay = functools.partial(relay_kernel, parts)
        first = to_owners(first, 1)
        over_y = [to_owners(wx, 2), to_owners(wy, 2)]
        over_x = []
        going = model[2:]
        for n in range(4):
            if n < 2:
                sent, going_on = call(
                    f"relay{n}",
                    relay,
                    (piece, piece),
                    [first, model[n], over_y[n], going[n]],
                )
                over_y.append(to_owners(going_on, 2))
            else:
                (sent,) = call(
                    f"relay{n}",
                    relay,
                    (piece,),
                    [first, model[n], over_y[n], (over_x[n - 2], HBM)],
                )
            over_x.append(to_owners(sent, 1))
        gathered = [[model[n], over_x[n], over_y[n]] for n in range(4)]
        after = sent
    else:
        slots = tuple(range(shots))
        gathered = [[a] + [to_owners(a, k) for k in range(1, shots)] for a in model]
        after = wx
    slope, src, inj, flags, matrix = prepare()

    edge = f32(4, width, depth)
    tensor, edge_a, edge_p = call(
        "window",
        functools.partial(window_kernel, slots, parts),
        (f32(2, rows, width, depth), f32(2, 4, width, depth), f32(2, 4, width, depth)),
        gathered[0] + gathered[1] + [flags],
    )
    edge_a = across_chips(edge_a)
    edge_p = to_partner(edge_p)
    last, flux, rest, last_a, last_p = call(
        "flux",
        functools.partial(flux_kernel, slots, parts),
        (field, field, field, edge, edge),
        gathered[2] + [flags, tensor, slope, matrix, (after, HBM)],
        scratch[2:3],
        work // 3,
    )
    last_a = across_chips(last_a)
    last_p = to_partner(last_p)

    speed, operand = call(
        "speed",
        functools.partial(speed_kernel, slots, parts),
        (field, field),
        gathered[3] + [flags, present],
    )
    op_a = across_chips(operand)
    op_p = to_partner(operand)

    image, following, coef = call(
        "forward0",
        forward_first,
        (field, field, f32(4, rows + 8, width, depth)),
        [tensor, edge_p, edge_a, last, last_p, last_a, slope, flux, rest]
        + [current, previous, speed, src],
        scratch[1:2],
        work // 4,
    )
    images = [image]
    previous, current = current, following
    adjoints = [present]
    known = None
    for t in range(STEPS - 1):
        now_a = across_chips(current)
        now_p = to_partner(current)
        back = STEPS - 1 - t
        ins = [operand, op_p, op_a, coef, matrix, present, later, inj, speed]
        outs = (field, field)
        if back == 1:
            ins = ins + [adjoints[1]] + images
            outs = (field, field, field)
        result = call(
            f"backward{t}", functools.partial(backward, back), outs, ins, scratch, work
        )
        later, present, operand = present, result[0], result[1]
        if back == 1:
            known = result[2]
        adjoints.append(present)
        op_a = across_chips(operand)
        op_p = to_partner(operand)
        if t < STEPS - 2:
            image, following = call(
                f"forward{t + 1}",
                functools.partial(forward, t + 1),
                (field, field),
                [current, now_p, now_a, coef, matrix, previous, speed, src],
                scratch,
                work,
            )
            images.append(image)
            previous, current = current, following

    chunks = call(
        "forward3",
        functools.partial(forward_last, parts),
        (f32(rows, count, depth),) * shots,
        [current, now_p, now_a, coef, matrix, known, adjoints[0], flags],
        scratch + (pltpu.VMEM((rows, width, depth), jnp.float32),),
        work,
    )
    received = [to_owners(chunks[k], k) for k in range(1, shots)]
    final, copied = call(
        "backward3",
        functools.partial(backward, 0),
        (field, field),
        [operand, op_p, op_a, coef, matrix, present, later, inj],
        scratch,
        work,
    )
    model_grad = call("total", total_kernel, piece, [chunks[0]] + received + [(final, HBM)])
    return (copied[None], final[None], model_grad)


def solution(mesh):
    in_specs = (
        P("shot", "blk", None, None),
        P("shot", "blk", None, None),
        P("shot", "blk", None, None),
        P("shot", "blk", None, None),
        P("blk", "shot", None),
        P("blk", "shot", None),
        P("blk", "shot", None),
        P("blk", "shot", None),
        P("shot"),
        P(),
        P("shot", None),
        P("shot", None, None),
        P("shot"),
        P("shot"),
        P("shot"),
        P("shot", None),
        P("shot", None),
        P("shot", None),
    )
    out_specs = (P("shot", "blk", None, None), P("shot", "blk", None, None), P("blk", "shot", None))
    return jax.shard_map(
        on_device, mesh=mesh, in_specs=in_specs, out_specs=out_specs, check_vma=False
    )
```

```python
import functools

import jax
import jax.numpy as jnp
from jax import lax
from jax.experimental import pallas as pl
from jax.experimental.pallas import tpu as pltpu
from jax.sharding import PartitionSpec as P

STEPS = 4
COEF = (0.8, -0.2, 4.0 / 105.0, -1.0 / 280.0)
WHOLE = (672.0, -168.0, 32.0, -3.0)
UNIT = 1.0 / 840.0
PAD = 8

VMEM = pl.BlockSpec(memory_space=pltpu.VMEM)
SMEM = pl.BlockSpec(memory_space=pltpu.SMEM)
HBM = pl.BlockSpec(memory_space=pltpu.HBM)


def f32(*shape):
    return jax.ShapeDtypeStruct(shape, jnp.float32)


def call(name, body, outs, ins, scratch=(), flops=1 << 20, moved=1 << 20):
    pairs = [a if isinstance(a, tuple) else (a, VMEM) for a in ins]
    return pl.pallas_call(
        body,
        name=name,
        out_shape=outs,
        in_specs=[s for _, s in pairs],
        out_specs=jax.tree.map(lambda _: VMEM, outs),
        scratch_shapes=list(scratch),
        cost_estimate=pl.CostEstimate(flops=flops, bytes_accessed=moved, transcendentals=0),
        compiler_params=pltpu.CompilerParams(vmem_limit_bytes=16 << 20),
    )(*[a for a, _ in pairs])


def stencil(pick):
    summed = None
    for k in range(1, 5):
        term = COEF[k - 1] * (pick(k) - pick(-k))
        summed = term if summed is None else summed + term
    return summed


def diff_y(ref, row, width):
    return stencil(lambda k: ref[row, PAD + k : PAD + k + width, :])


def diff_z(tile, matrix):
    high = tile.astype(jnp.bfloat16)
    low = (tile - high.astype(jnp.float32)).astype(jnp.bfloat16)
    both = jnp.concatenate([high, low], axis=-1)
    return jnp.dot(both, matrix[...], preferred_element_type=jnp.float32) * UNIT


def place_halos(wide, lane, own, partner, across):
    rows, halo = own.shape[0], sum(ref.shape[0] for ref in partner)
    blk, blocks = lax.axis_index("blk"), lax.axis_size("blk")
    odd = blk % 2
    outside = (blk == 0) | (blk == blocks - 1)
    above = halo + rows
    wide[(slice(halo, above), *lane)] = own[...]
    partner_at = jnp.where(odd == 1, 0, above)
    across_at = jnp.where(odd == 1, above, 0)
    for ref_p, ref_a in zip(partner, across):
        part = ref_p.shape[0]
        wide[(pl.ds(partner_at, part), *lane)] = ref_p[...]
        wide[(pl.ds(across_at, part), *lane)] = jnp.where(outside, 0.0, ref_a[...])
        partner_at, across_at = partner_at + part, across_at + part


def fill_field(own, partner, across, wide):
    rows, width, depth = own.shape
    edge = jnp.zeros((3 * rows, PAD, depth), jnp.float32)
    wide[:, 0:PAD, :] = edge
    wide[:, PAD + width : 2 * PAD + width, :] = edge
    place_halos(wide, (slice(PAD, PAD + width), slice(None)), own, (partner,), (across,))


def slopes_at(wide, i, width, matrix):
    inner = slice(PAD, PAD + width)
    return (
        stencil(lambda k: wide[i + k, inner, :]),
        diff_y(wide, i, width),
        diff_z(wide[i, inner, :], matrix),
    )


def clear_sides(flux_y, width):
    rows, _, depth = flux_y.shape
    edge = jnp.zeros((rows, PAD, depth), jnp.float32)
    flux_y[:, 0:PAD, :] = edge
    flux_y[:, PAD + width : 2 * PAD + width, :] = edge


def apply_operator(wide, coef, matrix, flux_x, flux_y, part_z, finish):
    rows, width, _ = part_z.shape
    clear_sides(flux_y, width)
    for i in range(rows + 8):
        slope_x, slope_y, slope_z = slopes_at(wide, i + 4, width, matrix)
        along = coef[0, i] * slope_x + coef[1, i] * slope_y + coef[2, i] * slope_z
        flux_x[i] = coef[3, i] * slope_x - coef[0, i] * along
        r = i - 4
        if 0 <= r < rows:
            flux_y[r, PAD : PAD + width, :] = coef[3, i] * slope_y - coef[1, i] * along
            part_z[r] = diff_z(coef[3, i] * slope_z - coef[2, i] * along, matrix)
    for r in range(rows):
        finish(r, stencil(lambda k: flux_x[r + 4 + k]) + diff_y(flux_y, r, width) + part_z[r])


def sin_cos(angle):
    square = angle * angle
    sine, cosine = 0.0, 1.0 / 479001600.0
    for factor in (-39916800.0, 362880.0, -5040.0, 120.0, -6.0, 1.0):
        sine = sine * square + 1.0 / factor
    for factor in (-3628800.0, 40320.0, -720.0, 24.0, -2.0, 1.0):
        cosine = cosine * square + 1.0 / factor
    return angle * sine, cosine


def owner_kernel(eps, tilt, azimuth, speed, state, wx, wy, wz, out, current, held, sems):
    rows = wx.shape[0]
    copies = [
        pltpu.make_async_copy(ref, to, sems.at[n])
        for n, (ref, to) in enumerate(
            (
                (eps, held.at[0]),
                (tilt, held.at[1]),
                (azimuth, held.at[2]),
                (speed, out),
                (state.at[0], current),
            )
        )
    ]
    for copy in copies:
        copy.start()
    for copy in copies[:3]:
        copy.wait()
    for r in range(rows):
        size = jnp.sqrt(2.0 * held[0, r])
        sin_tilt, cos_tilt = sin_cos(held[1, r])
        sin_half, cos_half = sin_cos(0.5 * held[2, r])
        flat = size * sin_tilt
        wx[r] = flat * (1.0 - 2.0 * sin_half * sin_half)
        wy[r] = flat * (2.0 * sin_half * cos_half)
        wz[r] = size * cos_tilt
    for copy in copies[3:]:
        copy.wait()


def first_kernel(anchor, wz, first, wz_first):
    rows, count, depth = wz.shape
    number = jnp.full((count, depth), (anchor[0] // count).astype(jnp.float32))
    first[...] = number[0:8]
    wz_first[0:rows] = wz[...]
    wz_first[rows] = number


def prepare_kernel(shots, parts, first, own, partner, across, slope, flags, matrix, wide):
    rows, width, depth = own.shape
    shape = matrix.shape
    offset = lax.broadcasted_iota(jnp.int32, shape, 0) % depth - lax.broadcasted_iota(
        jnp.int32, shape, 1
    )
    entries = jnp.zeros(shape, jnp.float32)
    for k in range(1, 5):
        entries = jnp.where(offset == k, WHOLE[k - 1], entries)
        entries = jnp.where(offset == -k, -WHOLE[k - 1], entries)
    matrix[...] = entries.astype(jnp.bfloat16)
    me = lax.axis_index("shot")
    for k in range(shots):
        part = jnp.bitwise_xor(me, k).astype(jnp.float32) - first[0:1, :]
        for j in range(parts):
            flags[k * parts + j : k * parts + j + 1, :] = jnp.where(
                jnp.abs(part - j) < 0.5, 1.0, 0.0
            )
    fill_field(own, partner, across, wide)
    for i in range(rows + 8):
        slope[0, i], slope[1, i], slope[2, i] = slopes_at(wide, i + 4, width, matrix)


def inject_kernel(numbers, wavelet, rx, ry, rz, traces, src, inj,
                  scalars, wave, receiver, samples_held, sems):
    rows, width, depth = src.shape[1:]
    copies = [
        pltpu.make_async_copy(numbers, scalars, sems.at[0]),
        pltpu.make_async_copy(wavelet, wave, sems.at[1]),
        pltpu.make_async_copy(traces, samples_held, sems.at[2]),
    ]
    for n, ref in enumerate((rx, ry, rz)):
        copies.append(pltpu.make_async_copy(ref, receiver[n], sems.at[3 + n]))
    for copy in copies:
        copy.start()
    for copy in copies:
        copy.wait()
    first = lax.axis_index("blk") * rows
    start = scalars[0]
    shape = (rows, width, depth)
    hit = (
        (lax.broadcasted_iota(jnp.int32, shape, 0) == scalars[1] - first)
        & (lax.broadcasted_iota(jnp.int32, shape, 1) == scalars[2])
        & (lax.broadcasted_iota(jnp.int32, shape, 2) == scalars[3])
    )
    moment = lax.broadcasted_iota(jnp.int32, wave.shape, 1)
    for t in range(STEPS - 1):
        value = jnp.sum(jnp.where(moment == start + t, wave[...], 0.0), axis=1, keepdims=True)
        src[t] = jnp.where(hit, value, 0.0)
    receivers = rx.shape[1]
    local = receiver[0][...] - first
    plane = jnp.where((local >= 0) & (local < rows), local * width + receiver[1][...], -1)
    pick = (
        lax.broadcasted_iota(jnp.int32, (rows * width, receivers), 0) == plane
    ).astype(jnp.float32)
    match = lax.broadcasted_iota(jnp.int32, (depth, receivers), 0) == receiver[2][...]
    for t in range(STEPS):
        samples = samples_held[0, pl.ds(start + t, 1), :]
        spread = jnp.where(match, samples, 0.0)
        added = lax.dot_general(
            pick,
            spread,
            (((1,), (1,)), ((), ())),
            precision=lax.Precision.HIGHEST,
            preferred_element_type=jnp.float32,
        )
        inj[t] = added.reshape(shape)


def relay_kernel(parts, wz_first, own, received, *refs):
    out = refs[-1]
    first = wz_first[wz_first.shape[0] - 1, 0:1, :]
    part = lax.axis_index("shot").astype(jnp.float32) - first
    inside = (part > -0.5) & (part < parts - 0.5)
    out[...] = jnp.where(inside, own[...], received[...])


def pair_kernel(own, received, out):
    out[0] = own[...]
    out[1] = received[0 : own.shape[0]]


def window_part(pieces, flags, parts, j):
    chosen = pieces[-1][...]
    for k in reversed(range(len(pieces) - 1)):
        at = k * parts + j
        chosen = jnp.where(flags[at : at + 1, :] > 0.5, pieces[k][...], chosen)
    return chosen


def piece_refs(refs, places):
    return [refs[i] if at is None else refs[i].at[at] for i, at in places]


def flux_kernel(places, parts, flags, slope, matrix, *refs):
    tensor, flux, rest, edge_a0, edge_a1, edge_p0, edge_p1, flux_y = refs[-8:]
    rows, width, _ = flux.shape
    count = width // parts
    for a in range(3):
        pieces = piece_refs(refs, places[a])
        for j in range(parts):
            tensor[a, :, j * count : (j + 1) * count, :] = window_part(pieces, flags, parts, j)
    odd = lax.axis_index("blk") % 2
    low = rows - 4
    for n, (out_a, out_p) in enumerate(((edge_a0, edge_p0), (edge_a1, edge_p1))):
        out_a[...] = tensor[:, pl.ds(odd * low + 2 * n, 2)]
        out_p[...] = tensor[:, pl.ds((1 - odd) * low + 2 * n, 2)]
    clear_sides(flux_y, width)
    for r in range(rows):
        wx, wy, wz = tensor[0, r], tensor[1, r], tensor[2, r]
        along = wx * slope[0, r + 4] + wy * slope[1, r + 4] + wz * slope[2, r + 4]
        size = 1.0 + (wx * wx + wy * wy + wz * wz)
        flux[r] = size * slope[0, r + 4] - wx * along
        flux_y[r, PAD : PAD + width, :] = size * slope[1, r + 4] - wy * along
        rest[r] = diff_z(size * slope[2, r + 4] - wz * along, matrix)
    for r in range(rows):
        rest[r] = rest[r] + diff_y(flux_y, r, width)


def speed_kernel(places, parts, flags, present, *refs):
    speed, operand = refs[-2:]
    pieces = piece_refs(refs, places)
    count = speed.shape[1] // parts
    for j in range(parts):
        speed[:, j * count : (j + 1) * count, :] = window_part(pieces, flags, parts, j)
    operand[...] = speed[...] * present[...]


def forward_first(tensor, edge_p0, edge_p1, edge_a0, edge_a1, slope, flux, rest, own, previous,
                  speed, src, image, following, coef, flux_x):
    rows = rest.shape[0]
    blk, blocks = lax.axis_index("blk"), lax.axis_size("blk")
    for a in range(3):
        place_halos(coef.at[a], (), tensor.at[a], (edge_p0.at[a], edge_p1.at[a]),
                    (edge_a0.at[a], edge_a1.at[a]))
    for i in range(rows + 8):
        wx, wy, wz = coef[0, i], coef[1, i], coef[2, i]
        size = 1.0 + (wx * wx + wy * wy + wz * wz)
        if i < 4:
            size = jnp.where(blk == 0, 0.0, size)
        if i >= rows + 4:
            size = jnp.where(blk == blocks - 1, 0.0, size)
        coef[3, i] = size
        if 4 <= i < rows + 4:
            flux_x[i] = flux[i - 4]
        else:
            along = wx * slope[0, i] + wy * slope[1, i] + wz * slope[2, i]
            flux_x[i] = size * slope[0, i] - wx * along
    for r in range(rows):
        value = stencil(lambda k: flux_x[r + 4 + k]) + rest[r]
        image[r] = value
        following[r] = 2.0 * own[r] - previous[r] + speed[r] * value + src[0, r]


def forward(t, own, partner, across, coef, matrix, previous, speed, src, image, following,
            wide, *scratch):
    fill_field(own, partner, across, wide)

    def finish(r, value):
        image[r] = value
        following[r] = 2.0 * own[r] - previous[r] + speed[r] * value + src[t, r]

    apply_operator(wide, coef, matrix, *scratch, finish)


def backward(t, own, partner, across, coef, matrix, present, later, inj, *refs):
    if t == 0:
        earlier, copied, done = refs[:3]
        copied[...] = present[...]
        done[...] = jnp.zeros(done.shape, jnp.float32)
    elif t == 1:
        speed, lambda3, image0, image1, image2, earlier, operand, known = refs[:8]
    else:
        speed, earlier, operand = refs[:3]
    wide, flux_x, flux_y, part_z = refs[-4:]
    fill_field(own, partner, across, wide)

    def finish(r, value):
        result = 2.0 * present[r] - later[r] + value + inj[t, r]
        earlier[r] = result
        if t > 0:
            operand[r] = speed[r] * result
        if t == 1:
            known[r] = lambda3[r] * image2[r] + present[r] * image1[r] + result * image0[r]

    apply_operator(wide, coef, matrix, flux_x, flux_y, part_z, finish)


def forward_last(parts, own, partner, across, coef, matrix, known, lambda4, flags, *refs):
    *chunks, wide, flux_x, flux_y, part_z, grad = refs
    count = chunks[0].shape[1]
    fill_field(own, partner, across, wide)

    def finish(r, value):
        grad[r] = known[r] + lambda4[r] * value

    apply_operator(wide, coef, matrix, flux_x, flux_y, part_z, finish)
    for k, chunk in enumerate(chunks):
        held = jnp.zeros(chunk.shape, jnp.float32)
        for j in range(parts):
            at = k * parts + j
            held = jnp.where(
                flags[at : at + 1, :] > 0.5, grad[:, j * count : (j + 1) * count, :], held
            )
        chunk[...] = held


def total_kernel(*refs):
    out = refs[-1]
    total = refs[0][...]
    for ref in refs[1:-2]:
        total = total + ref[...]
    out[...] = total


def on_device(
    state_before,
    state_now,
    adjoint_later,
    adjoint_now,
    courant_sq,
    epsilon,
    tilt_angle,
    azimuth,
    aperture_anchor,
    step_index,
    wavelet,
    residual_traces,
    source_x,
    source_y,
    source_z,
    receiver_x,
    receiver_y,
    receiver_z,
):
    rows, width, depth = state_now.shape[1:]
    count = courant_sq.shape[1]
    parts = width // count
    shots = lax.axis_size("shot")
    blocks = lax.axis_size("blk")
    field, piece = f32(rows, width, depth), f32(rows, count, depth)
    wide = (rows, width + 2 * PAD, depth)
    scratch = (
        pltpu.VMEM((3 * rows, width + 2 * PAD, depth), jnp.float32),
        pltpu.VMEM((rows + 8, width, depth), jnp.float32),
        pltpu.VMEM(wide, jnp.float32),
        pltpu.VMEM((rows, width, depth), jnp.float32),
    )
    work = 100 * (rows + 8) * width * depth

    core_pairs = [(i, i ^ 1) for i in range(blocks)]
    chip_pairs = []
    for s in range(shots):
        for b in range(blocks):
            end = b in (0, blocks - 1)
            other = (s ^ 1, b) if end else (s, b - 1 + 2 * (b % 2))
            chip_pairs.append((s * blocks + b, other[0] * blocks + other[1]))

    def to_partner(array):
        return lax.ppermute(array, "blk", core_pairs)

    def across_chips(array):
        return lax.ppermute(array, ("shot", "blk"), chip_pairs)

    def halos(array):
        return to_partner(array), across_chips(array)

    def in_hbm(array):
        return pltpu.with_memory_space_constraint(array, pltpu.HBM), HBM

    def to_owners(array, k):
        return lax.ppermute(array, "shot", [(i, i ^ k) for i in range(shots)])

    previous = state_before[0]
    present, later = adjoint_now[0], adjoint_later[0]

    wx, wy, wz, speed, current = call(
        "owner",
        owner_kernel,
        (piece,) * 4 + (field,),
        [in_hbm(a) for a in (epsilon, tilt_angle, azimuth, courant_sq, state_now)],
        (
            pltpu.VMEM((3, rows, count, depth), jnp.float32),
            pltpu.SemaphoreType.DMA((5,)),
        ),
    )
    first, wz_first = call(
        "first",
        first_kernel,
        (f32(8, depth), f32(rows + 1, count, depth)),
        [(aperture_anchor, SMEM), wz],
    )

    if shots == 4 and parts == 2:
        relay = functools.partial(relay_kernel, parts)
        wx_y = to_owners(wx, 2)
        wz_x = to_owners(wz_first, 1)
        wy_y = to_owners(wy, 2)
        speed_x = to_owners(speed, 1)
        wx_sent = call("relay_wx", relay, piece, [wz_x, wx, wx_y])
        wx_x = to_owners(wx_sent, 1)
        both = f32(2, rows, count, depth)
        wz_y = to_owners(call("pair_wz", pair_kernel, both, [wz, wz_x]), 2)
        wy_sent = call("relay_wy", relay, piece, [wz_x, wy, wy_y, speed_x, wx_sent])
        wy_x = to_owners(wy_sent, 1)
        speed_y = to_owners(call("pair_speed", pair_kernel, both, [speed, speed_x]), 2)
        pieces = [wx, wx_x, wx_y, wy, wy_x, wy_y, wz, wz_x, wz_y]
        places = [
            [(0, None), (1, None), (2, None), (1, None)],
            [(3, None), (4, None), (5, None), (4, None)],
            [(6, None), (7, slice(0, rows)), (8, 0), (8, 1)],
        ]
        speed_pieces = [speed, speed_x, speed_y]
        speed_places = [(0, None), (1, None), (2, 0), (2, 1)]
    else:
        pieces, places = [], []
        for array in (wx, wy, wz):
            places.append([(len(pieces) + k, None) for k in range(shots)])
            pieces = pieces + [array] + [to_owners(array, k) for k in range(1, shots)]
        speed_places = places[0]
        speed_pieces = [speed] + [to_owners(speed, k) for k in range(1, shots)]

    now_p, now_a = halos(current)
    slope, flags, matrix = call(
        "prepare",
        functools.partial(prepare_kernel, shots, parts),
        (
            f32(3, rows + 8, width, depth),
            f32(shots * parts, depth),
            jax.ShapeDtypeStruct((2 * depth, depth), jnp.bfloat16),
        ),
        [first, current, now_p, now_a],
        scratch[:1],
    )
    edge = f32(3, 2, width, depth)
    tensor, flux, rest, *edges = call(
        "flux",
        functools.partial(flux_kernel, places, parts),
        (f32(3, rows, width, depth), field, field, edge, edge, edge, edge),
        [flags, slope, matrix] + pieces,
        scratch[2:3],
        work // 3,
    )
    edges_a = [across_chips(a) for a in edges[:2]]
    edges_p = [to_partner(a) for a in edges[2:]]

    speed, operand = call(
        "speed",
        functools.partial(speed_kernel, speed_places, parts),
        (field, field),
        [flags, present] + speed_pieces,
    )
    op_p, op_a = halos(operand)

    numbers = jnp.concatenate([step_index, source_x, source_y, source_z])
    src, inj = call(
        "inject",
        inject_kernel,
        (f32(STEPS - 1, rows, width, depth), f32(STEPS, rows, width, depth)),
        [
            in_hbm(a)
            for a in (numbers, wavelet, receiver_x, receiver_y, receiver_z, residual_traces)
        ],
        (
            pltpu.SMEM((4,), jnp.int32),
            pltpu.VMEM(wavelet.shape, jnp.float32),
            [pltpu.VMEM(receiver_x.shape, jnp.int32)] * 3,
            pltpu.VMEM(residual_traces.shape, jnp.float32),
            pltpu.SemaphoreType.DMA((6,)),
        ),
        1 << 28,
        1,
    )
    image, following, coef = call(
        "forward0",
        forward_first,
        (field, field, f32(4, rows + 8, width, depth)),
        [tensor, *edges_p, *edges_a, slope, flux, rest]
        + [current, previous, speed, src],
        scratch[1:2],
        work // 4,
    )
    images = [image]
    previous, current = current, following
    adjoints = [present]
    known = None
    for t in range(STEPS - 1):
        now_p, now_a = halos(current)
        back = STEPS - 1 - t
        ins = [operand, op_p, op_a, coef, matrix, present, later, inj, speed]
        outs = (field, field)
        if back == 1:
            ins = ins + [adjoints[1]] + images
            outs = (field, field, field)
        result = call(
            f"backward{t}", functools.partial(backward, back), outs, ins, scratch, work
        )
        later, present, operand = present, result[0], result[1]
        if back == 1:
            known = result[2]
        adjoints.append(present)
        op_p, op_a = halos(operand)
        if t < STEPS - 2:
            image, following = call(
                f"forward{t + 1}",
                functools.partial(forward, t + 1),
                (field, field),
                [current, now_p, now_a, coef, matrix, previous, speed, src],
                scratch,
                work,
            )
            images.append(image)
            previous, current = current, following

    chunks = call(
        "forward3",
        functools.partial(forward_last, parts),
        (f32(rows, count, depth),) * shots,
        [current, now_p, now_a, coef, matrix, known, adjoints[0], flags],
        scratch + (pltpu.VMEM((rows, width, depth), jnp.float32),),
        work,
    )
    received = [to_owners(chunks[k], k) for k in range(1, shots)]
    final, copied, done = call(
        "backward3",
        functools.partial(backward, 0),
        (field, field, f32(8, depth)),
        [operand, op_p, op_a, coef, matrix, present, later, inj],
        scratch,
        work,
    )
    model_grad = call("total", total_kernel, piece, [chunks[0]] + received + [done])
    return (copied[None], final[None], model_grad)


def solution(mesh):
    in_specs = (
        P("shot", "blk", None, None),
        P("shot", "blk", None, None),
        P("shot", "blk", None, None),
        P("shot", "blk", None, None),
        P("blk", "shot", None),
        P("blk", "shot", None),
        P("blk", "shot", None),
        P("blk", "shot", None),
        P("shot"),
        P(),
        P("shot", None),
        P("shot", None, None),
        P("shot"),
        P("shot"),
        P("shot"),
        P("shot", None),
        P("shot", None),
        P("shot", None),
    )
    out_specs = (P("shot", "blk", None, None), P("shot", "blk", None, None), P("blk", "shot", None))
    return jax.shard_map(
        on_device, mesh=mesh, in_specs=in_specs, out_specs=out_specs, check_vma=False
    )
```

```python
import functools

import jax
import jax.numpy as jnp
from jax import lax
from jax.experimental import pallas as pl
from jax.experimental.pallas import tpu as pltpu
from jax.sharding import PartitionSpec as P

STEPS = 4
COEF = (0.8, -0.2, 4.0 / 105.0, -1.0 / 280.0)
WHOLE = (672.0, -168.0, 32.0, -3.0)
UNIT = 1.0 / 840.0

VMEM = pl.BlockSpec(memory_space=pltpu.VMEM)
SMEM = pl.BlockSpec(memory_space=pltpu.SMEM)
HBM = pl.BlockSpec(memory_space=pltpu.HBM)


def f32(*shape):
    return jax.ShapeDtypeStruct(shape, jnp.float32)


def call(name, body, outs, ins, scratch=(), flops=1 << 20, moved=1 << 20):
    pairs = [a if isinstance(a, tuple) else (a, VMEM) for a in ins]
    return pl.pallas_call(
        body,
        name=name,
        out_shape=outs,
        in_specs=[s for _, s in pairs],
        out_specs=jax.tree.map(lambda _: VMEM, outs),
        scratch_shapes=list(scratch),
        cost_estimate=pl.CostEstimate(flops=flops, bytes_accessed=moved, transcendentals=0),
        compiler_params=pltpu.CompilerParams(vmem_limit_bytes=16 << 20),
    )(*[a for a, _ in pairs])


def stencil(pick):
    summed = None
    for k in range(1, 5):
        term = COEF[k - 1] * (pick(k) - pick(-k))
        summed = term if summed is None else summed + term
    return summed


def halves(tile):
    high = tile.astype(jnp.bfloat16)
    return high, (tile - high.astype(jnp.float32)).astype(jnp.bfloat16)


def diff_z(tile, matrix):
    return jnp.dot(
        jnp.concatenate(halves(tile), axis=1), matrix[...], preferred_element_type=jnp.float32
    )


def diff_y(tile, matrix):
    return jnp.dot(
        matrix[...], jnp.concatenate(halves(tile), axis=0), preferred_element_type=jnp.float32
    )


def diff_matrix(size, along, shape):
    row = lax.broadcasted_iota(jnp.int32, shape, 0) % size
    column = lax.broadcasted_iota(jnp.int32, shape, 1) % size
    offset = row - column if along == 0 else column - row
    entries = jnp.zeros(shape, jnp.float32)
    for k in range(1, 5):
        entries = jnp.where(offset == k, WHOLE[k - 1], entries)
        entries = jnp.where(offset == -k, -WHOLE[k - 1], entries)
    return entries.astype(jnp.bfloat16)


def place_halos(wide, own, partner, across):
    rows, halo = own.shape[0], sum(ref.shape[0] for ref in partner)
    blk, blocks = lax.axis_index("blk"), lax.axis_size("blk")
    odd = blk % 2
    outside = (blk == 0) | (blk == blocks - 1)
    above = halo + rows
    wide[halo:above] = own[...]
    partner_at = jnp.where(odd == 1, 0, above)
    across_at = jnp.where(odd == 1, above, 0)
    for ref_p, ref_a in zip(partner, across):
        part = ref_p.shape[0]
        wide[pl.ds(partner_at, part)] = ref_p[...]
        wide[pl.ds(across_at, part)] = jnp.where(outside, 0.0, ref_a[...])
        partner_at, across_at = partner_at + part, across_at + part


def slopes_yz(wide, first, out_y, out_z, matrix_y, matrix_z):
    for i in range(out_z.shape[0]):
        out_z[i] = diff_z(wide[first + i] * UNIT, matrix_z)
    for i in range(out_y.shape[0]):
        out_y[i] = diff_y(wide[first + i] * UNIT, matrix_y)


def apply_operator(halos, coef, matrix_y, matrix_z, scratch, finish):
    wide, flux_x, all_y, all_z, part = scratch
    rows = part.shape[0]
    own, partner, across = halos
    place_halos(wide, own, (partner,), (across,))
    slopes_yz(wide, 4, all_y, all_z, matrix_y, matrix_z)
    for i in range(rows + 8):
        slope_x = stencil(lambda k: wide[i + 4 + k])
        slope_y, slope_z = all_y[i], all_z[i]
        along = coef[0, i] * slope_x + coef[1, i] * slope_y + coef[2, i] * slope_z
        flux_x[i] = coef[3, i] * slope_x - coef[0, i] * along
        if 4 <= i < rows + 4:
            part[i - 4] = UNIT * (
                diff_z(coef[3, i] * slope_z - coef[2, i] * along, matrix_z)
                + diff_y(coef[3, i] * slope_y - coef[1, i] * along, matrix_y)
            )
    for r in range(rows):
        finish(r, stencil(lambda k: flux_x[r + 4 + k]) + part[r])


def sin_cos(angle):
    square = angle * angle
    sine, cosine = 0.0, 1.0 / 479001600.0
    for factor in (-39916800.0, 362880.0, -5040.0, 120.0, -6.0, 1.0):
        sine = sine * square + 1.0 / factor
    for factor in (-3628800.0, 40320.0, -720.0, 24.0, -2.0, 1.0):
        cosine = cosine * square + 1.0 / factor
    return angle * sine, cosine


def owner_kernel(eps, tilt, azimuth, speed, state, wx, wy, wz, out, current, held, sems):
    rows = wx.shape[0]
    copies = [
        pltpu.make_async_copy(ref, to, sems.at[n])
        for n, (ref, to) in enumerate(
            (
                (eps, held.at[0]),
                (tilt, held.at[1]),
                (azimuth, held.at[2]),
                (speed, out),
                (state.at[0], current),
            )
        )
    ]
    for copy in copies:
        copy.start()
    for copy in copies[:3]:
        copy.wait()
    for r in range(rows):
        size = jnp.sqrt(2.0 * held[0, r])
        sin_tilt, cos_tilt = sin_cos(held[1, r])
        sin_half, cos_half = sin_cos(0.5 * held[2, r])
        flat = size * sin_tilt
        wx[r] = flat * (1.0 - 2.0 * sin_half * sin_half)
        wy[r] = flat * (2.0 * sin_half * cos_half)
        wz[r] = size * cos_tilt
    for copy in copies[3:]:
        copy.wait()


def first_kernel(anchor, wz, first, wz_first):
    rows, count, depth = wz.shape
    number = (anchor[...].reshape(1, 1) // count).astype(jnp.float32)
    number = jnp.broadcast_to(number, (count, depth))
    first[...] = number[0:8]
    wz_first[0:rows] = wz[...]
    wz_first[rows] = number


def prepare_kernel(shots, parts, first, own, partner, across, *refs):
    slope, flags, matrix_y, matrix_z, wide = refs[-5:]
    rows, width, depth = own.shape
    matrix_y[...] = diff_matrix(width, 1, matrix_y.shape)
    matrix_z[...] = diff_matrix(depth, 0, matrix_z.shape)
    me = lax.axis_index("shot")
    for k in range(shots):
        part = jnp.bitwise_xor(me, k).astype(jnp.float32) - first[0:1, :]
        for j in range(parts):
            flags[k * parts + j : k * parts + j + 1, :] = jnp.where(
                jnp.abs(part - j) < 0.5, 1.0, 0.0
            )
    place_halos(wide, own, (partner,), (across,))
    slopes_yz(wide, 4, slope.at[1], slope.at[2], matrix_y, matrix_z)
    for i in range(rows + 8):
        slope[0, i] = stencil(lambda k: wide[i + 4 + k])


def inject_kernel(step, sx, sy, sz, wavelet, rx, ry, rz, traces, src, inj):
    rows, width, depth = src.shape[1:]
    start, sx, sy, sz = (ref[...].reshape(1, 1) for ref in (step, sx, sy, sz))
    first = lax.axis_index("blk") * rows
    shape = (rows, width, depth)
    plane = (width, depth)
    here = (lax.broadcasted_iota(jnp.int32, plane, 0) == sy) & (
        lax.broadcasted_iota(jnp.int32, plane, 1) == sz
    )
    moment = lax.broadcasted_iota(jnp.int32, wavelet.shape, 1)
    for t in range(STEPS - 1):
        chosen = jnp.where(moment == start + t, wavelet[...], 0.0)
        value = jnp.sum(chosen, axis=1, keepdims=True)
        for r in range(rows):
            src[t, r] = jnp.where(here & (sx == first + r), value, 0.0)
    receivers = rx.shape[1]
    local = rx[...] - first
    cell = jnp.where((local >= 0) & (local < rows), local * width + ry[...], -1)
    pick = (
        lax.broadcasted_iota(jnp.int32, (rows * width, receivers), 0) == cell
    ).astype(jnp.float32)
    match = lax.broadcasted_iota(jnp.int32, (depth, receivers), 0) == rz[...]
    moment = lax.broadcasted_iota(jnp.int32, traces.shape[1:], 0)
    for t in range(STEPS):
        chosen = jnp.where(moment == start + t, traces[0], 0.0)
        samples = jnp.sum(chosen, axis=0, keepdims=True)
        spread = jnp.where(match, samples, 0.0)
        added = lax.dot_general(
            pick,
            spread,
            (((1,), (1,)), ((), ())),
            precision=lax.Precision.HIGHEST,
            preferred_element_type=jnp.float32,
        )
        inj[t] = added.reshape(shape)


def relay_kernel(parts, wz_first, own, received, *refs):
    out = refs[-1]
    first = wz_first[wz_first.shape[0] - 1, 0:1, :]
    part = lax.axis_index("shot").astype(jnp.float32) - first
    inside = (part > -0.5) & (part < parts - 0.5)
    out[...] = jnp.where(inside, own[...], received[...])


def pair_kernel(own, received, out):
    out[0] = own[...]
    out[1] = received[0 : own.shape[0]]


def window_part(pieces, flags, parts, j):
    chosen = pieces[-1][...]
    for k in reversed(range(len(pieces) - 1)):
        at = k * parts + j
        chosen = jnp.where(flags[at : at + 1, :] > 0.5, pieces[k][...], chosen)
    return chosen


def piece_refs(refs, places):
    return [refs[i] if at is None else refs[i].at[at] for i, at in places]


def flux_kernel(places, parts, flags, slope, matrix_y, matrix_z, *refs):
    tensor, flux, rest, edge_a0, edge_a1, edge_p0, edge_p1 = refs[-7:]
    rows, width, _ = flux.shape
    count = width // parts
    for a in range(3):
        pieces = piece_refs(refs, places[a])
        for j in range(parts):
            tensor[a, :, j * count : (j + 1) * count, :] = window_part(pieces, flags, parts, j)
    odd = lax.axis_index("blk") % 2
    low = rows - 4
    for n, (out_a, out_p) in enumerate(((edge_a0, edge_p0), (edge_a1, edge_p1))):
        out_a[...] = tensor[:, pl.ds(odd * low + 2 * n, 2)]
        out_p[...] = tensor[:, pl.ds((1 - odd) * low + 2 * n, 2)]
    for r in range(rows):
        wx, wy, wz = tensor[0, r], tensor[1, r], tensor[2, r]
        along = wx * slope[0, r + 4] + wy * slope[1, r + 4] + wz * slope[2, r + 4]
        size = 1.0 + (wx * wx + wy * wy + wz * wz)
        flux[r] = size * slope[0, r + 4] - wx * along
        rest[r] = UNIT * (
            diff_z(size * slope[2, r + 4] - wz * along, matrix_z)
            + diff_y(size * slope[1, r + 4] - wy * along, matrix_y)
        )


def speed_kernel(places, parts, flags, present, *refs):
    speed, operand = refs[-2:]
    pieces = piece_refs(refs, places)
    count = speed.shape[1] // parts
    for j in range(parts):
        speed[:, j * count : (j + 1) * count, :] = window_part(pieces, flags, parts, j)
    operand[...] = speed[...] * present[...]


def forward_first(tensor, edge_p0, edge_p1, edge_a0, edge_a1, slope, flux, rest, own, previous, speed, src,
                  image, following, coef, flux_x):
    rows = rest.shape[0]
    blk, blocks = lax.axis_index("blk"), lax.axis_size("blk")
    for a in range(3):
        place_halos(coef.at[a], tensor.at[a], (edge_p0.at[a], edge_p1.at[a]),
                    (edge_a0.at[a], edge_a1.at[a]))
    for i in range(rows + 8):
        wx, wy, wz = coef[0, i], coef[1, i], coef[2, i]
        size = 1.0 + (wx * wx + wy * wy + wz * wz)
        if i < 4:
            size = jnp.where(blk == 0, 0.0, size)
        if i >= rows + 4:
            size = jnp.where(blk == blocks - 1, 0.0, size)
        coef[3, i] = size
        if 4 <= i < rows + 4:
            flux_x[i] = flux[i - 4]
        else:
            along = wx * slope[0, i] + wy * slope[1, i] + wz * slope[2, i]
            flux_x[i] = size * slope[0, i] - wx * along
    for r in range(rows):
        value = stencil(lambda k: flux_x[r + 4 + k]) + rest[r]
        image[r] = value
        following[r] = 2.0 * own[r] - previous[r] + speed[r] * value + src[0, r]


def forward(t, own, across, partner, coef, matrix_y, matrix_z, previous, speed, src,
            image, following, *scratch):
    def finish(r, value):
        image[r] = value
        following[r] = 2.0 * own[r] - previous[r] + speed[r] * value + src[t, r]

    apply_operator((own, partner, across), coef, matrix_y, matrix_z, scratch, finish)


def backward(t, own, across, partner, coef, matrix_y, matrix_z, present, later, inj, *refs):
    refs, scratch = refs[:-5], refs[-5:]
    if t == 0:
        earlier, copied, done = refs
        copied[...] = present[...]
        done[...] = jnp.zeros(done.shape, jnp.float32)
    elif t == 1:
        speed, lambda3, image0, image1, image2, earlier, operand, known = refs
    else:
        speed, earlier, operand = refs

    def finish(r, value):
        result = 2.0 * present[r] - later[r] + value + inj[t, r]
        earlier[r] = result
        if t > 0:
            operand[r] = speed[r] * result
        if t == 1:
            known[r] = lambda3[r] * image2[r] + present[r] * image1[r] + result * image0[r]

    apply_operator((own, partner, across), coef, matrix_y, matrix_z, scratch, finish)


def forward_last(parts, own, across, partner, coef, matrix_y, matrix_z, known, lambda4, flags,
                 *refs):
    chunks, scratch, grad = refs[:-6], refs[-6:-1], refs[-1]
    count = chunks[0].shape[1]

    def finish(r, value):
        grad[r] = known[r] + lambda4[r] * value

    apply_operator((own, partner, across), coef, matrix_y, matrix_z, scratch, finish)
    for k, chunk in enumerate(chunks):
        held = jnp.zeros(chunk.shape, jnp.float32)
        for j in range(parts):
            at = k * parts + j
            held = jnp.where(
                flags[at : at + 1, :] > 0.5, grad[:, j * count : (j + 1) * count, :], held
            )
        chunk[...] = held


def total_kernel(*refs):
    out = refs[-1]
    total = refs[0][...]
    for ref in refs[1:-2]:
        total = total + ref[...]
    out[...] = total


def on_device(
    state_before,
    state_now,
    adjoint_later,
    adjoint_now,
    courant_sq,
    epsilon,
    tilt_angle,
    azimuth,
    aperture_anchor,
    step_index,
    wavelet,
    residual_traces,
    source_x,
    source_y,
    source_z,
    receiver_x,
    receiver_y,
    receiver_z,
):
    rows, width, depth = state_now.shape[1:]
    count = courant_sq.shape[1]
    parts = width // count
    shots = lax.axis_size("shot")
    blocks = lax.axis_size("blk")
    field, piece = f32(rows, width, depth), f32(rows, count, depth)
    extended = pltpu.VMEM((rows + 8, width, depth), jnp.float32)
    wide = pltpu.VMEM((3 * rows, width, depth), jnp.float32)
    own_rows = pltpu.VMEM((rows, width, depth), jnp.float32)
    scratch = (wide, extended, extended, extended, own_rows)
    work = 100 * (rows + 8) * width * depth

    core_pairs = [(i, i ^ 1) for i in range(blocks)]
    def chip_pairs(hop):
        pairs = []
        for s in range(shots):
            for b in range(blocks):
                end = b in (0, blocks - 1)
                other = (s ^ hop, b) if end else (s, b - 1 + 2 * (b % 2))
                pairs.append((s * blocks + b, other[0] * blocks + other[1]))
        return pairs

    def to_partner(array, name):
        with jax.named_scope(f"{name}_to_core"):
            return lax.ppermute(array, "blk", core_pairs)

    def across_chips(array, name, hop=2):
        with jax.named_scope(f"{name}_to_chip"):
            return lax.ppermute(array, ("shot", "blk"), chip_pairs(hop))

    def halos(array, name):
        return to_partner(array, name), across_chips(array, name)

    def in_hbm(array):
        return pltpu.with_memory_space_constraint(array, pltpu.HBM), HBM

    def to_owners(array, k, name):
        with jax.named_scope(f"{name}_to_{k}"):
            return lax.ppermute(array, "shot", [(i, i ^ k) for i in range(shots)])

    previous = state_before[0]
    present, later = adjoint_now[0], adjoint_later[0]

    wx, wy, wz, speed, current = call(
        "owner",
        owner_kernel,
        (piece,) * 4 + (field,),
        [in_hbm(a) for a in (epsilon, tilt_angle, azimuth, courant_sq, state_now)],
        (
            pltpu.VMEM((3, rows, count, depth), jnp.float32),
            pltpu.SemaphoreType.DMA((5,)),
        ),
    )
    first, wz_first = call(
        "first",
        first_kernel,
        (f32(8, depth), f32(rows + 1, count, depth)),
        [aperture_anchor, wz],
    )

    if shots == 4 and parts == 2:
        relay = functools.partial(relay_kernel, parts)
        wx_y = to_owners(wx, 2, "wx")
        wz_x = to_owners(wz_first, 1, "wz")
        wy_y = to_owners(wy, 2, "wy")
        wx_sent = call("relay_wx", relay, piece, [wz_x, wx, wx_y])
        wx_x = to_owners(wx_sent, 1, "wx")
        both = f32(2, rows, count, depth)
        wz_y = to_owners(call("pair_wz", pair_kernel, both, [wz, wz_x]), 2, "wz")
        wy_sent = call("relay_wy", relay, piece, [wz_x, wy, wy_y, wx_sent])
        wy_x = to_owners(wy_sent, 1, "wy")
        speed_x = to_owners(speed, 1, "speed")
        speed_y = to_owners(call("pair_speed", pair_kernel, both, [speed, speed_x]), 2, "speed")
        before = [wx_x, speed_x]
        pieces = [wx, wx_x, wx_y, wy, wy_x, wy_y, wz, wz_x, wz_y]
        places = [
            [(0, None), (1, None), (2, None), (1, None)],
            [(3, None), (4, None), (5, None), (4, None)],
            [(6, None), (7, slice(0, rows)), (8, 0), (8, 1)],
        ]
        speed_pieces = [speed, speed_x, speed_y]
        speed_places = [(0, None), (1, None), (2, 0), (2, 1)]
    else:
        pieces, places, before = [], [], []
        for array in (wx, wy, wz):
            places.append([(len(pieces) + k, None) for k in range(shots)])
            pieces = pieces + [array] + [to_owners(array, k, "w") for k in range(1, shots)]
        speed_places = places[0]
        speed_pieces = [speed] + [to_owners(speed, k, "speed") for k in range(1, shots)]

    src, inj = call(
        "inject",
        inject_kernel,
        (f32(STEPS - 1, rows, width, depth), f32(STEPS, rows, width, depth)),
        [step_index, source_x, source_y, source_z, wavelet, receiver_x, receiver_y, receiver_z]
        + [residual_traces],
    )
    now_p, now_a = to_partner(current, "state"), across_chips(current, "state", 1)
    slope, flags, matrix_y, matrix_z = call(
        "prepare",
        functools.partial(prepare_kernel, shots, parts),
        (
            f32(3, rows + 8, width, depth),
            f32(shots * parts, depth),
            jax.ShapeDtypeStruct((width, 2 * width), jnp.bfloat16),
            jax.ShapeDtypeStruct((2 * depth, depth), jnp.bfloat16),
        ),
        [first, current, now_p, now_a, src] + before,
        [wide],
    )
    edge = f32(3, 2, width, depth)
    tensor, flux, rest, *edges = call(
        "flux",
        functools.partial(flux_kernel, places, parts),
        (f32(3, rows, width, depth), field, field) + (edge,) * 4,
        [flags, slope, matrix_y, matrix_z] + pieces,
        flops=work // 3,
    )
    edges_a = [across_chips(a, "edge") for a in edges[:2]]
    edges_p = [to_partner(a, "edge") for a in edges[2:]]
    speed, operand = call(
        "speed",
        functools.partial(speed_kernel, speed_places, parts),
        (field, field),
        [flags, present] + speed_pieces,
    )
    op_p, op_a = halos(operand, "adjoint")

    image, following, coef = call(
        "forward0",
        forward_first,
        (field, field, f32(4, rows + 8, width, depth)),
        [tensor, *edges_p, *edges_a, slope, flux, rest]
        + [current, previous, speed, src],
        [extended],
        work // 4,
    )
    images = [image]
    previous, current = current, following
    adjoints = [present]
    known = None
    for t in range(STEPS - 1):
        now_p, now_a = halos(current, "state")
        back = STEPS - 1 - t
        ins = [operand, op_a, op_p, coef, matrix_y, matrix_z, present, later, inj, speed]
        outs = (field, field)
        if back == 1:
            ins = ins + [adjoints[1]] + images
            outs = (field, field, field)
        result = call(
            f"backward{t}", functools.partial(backward, back), outs, ins, scratch, work
        )
        later, present, operand = present, result[0], result[1]
        if back == 1:
            known = result[2]
        adjoints.append(present)
        op_p, op_a = halos(operand, "adjoint")
        if t < STEPS - 2:
            image, following = call(
                f"forward{t + 1}",
                functools.partial(forward, t + 1),
                (field, field),
                [current, now_a, now_p, coef, matrix_y, matrix_z, previous, speed, src],
                scratch,
                work,
            )
            images.append(image)
            previous, current = current, following

    chunks = call(
        "forward3",
        functools.partial(forward_last, parts),
        (piece,) * shots,
        [current, now_a, now_p, coef, matrix_y, matrix_z, known, adjoints[0], flags],
        scratch + (own_rows,),
        work,
    )
    received = [to_owners(chunks[k], k, "grad") for k in range(1, shots)]
    final, copied, done = call(
        "backward3",
        functools.partial(backward, 0),
        (field, field, f32(8, depth)),
        [operand, op_a, op_p, coef, matrix_y, matrix_z, present, later, inj],
        scratch,
        work,
    )
    model_grad = call("total", total_kernel, piece, [chunks[0]] + received + [done])
    return (copied[None], final[None], model_grad)


def solution(mesh):
    in_specs = (
        P("shot", "blk", None, None),
        P("shot", "blk", None, None),
        P("shot", "blk", None, None),
        P("shot", "blk", None, None),
        P("blk", "shot", None),
        P("blk", "shot", None),
        P("blk", "shot", None),
        P("blk", "shot", None),
        P("shot"),
        P(),
        P("shot", None),
        P("shot", None, None),
        P("shot"),
        P("shot"),
        P("shot"),
        P("shot", None),
        P("shot", None),
        P("shot", None),
    )
    out_specs = (P("shot", "blk", None, None), P("shot", "blk", None, None), P("blk", "shot", None))
    return jax.shard_map(
        on_device, mesh=mesh, in_specs=in_specs, out_specs=out_specs, check_vma=False
    )
```

```python
import functools

import jax
import jax.numpy as jnp
from jax import lax
from jax.experimental import pallas as pl
from jax.experimental.pallas import tpu as pltpu
from jax.sharding import PartitionSpec as P

STEPS = 4
COEF = (0.8, -0.2, 4.0 / 105.0, -1.0 / 280.0)
WHOLE = (672.0, -168.0, 32.0, -3.0)
UNIT = 1.0 / 840.0

VMEM = pl.BlockSpec(memory_space=pltpu.VMEM)
SMEM = pl.BlockSpec(memory_space=pltpu.SMEM)
HBM = pl.BlockSpec(memory_space=pltpu.HBM)


def f32(*shape):
    return jax.ShapeDtypeStruct(shape, jnp.float32)


def call(name, body, outs, ins, scratch=(), flops=1 << 20, moved=1 << 20):
    pairs = [a if isinstance(a, tuple) else (a, VMEM) for a in ins]
    return pl.pallas_call(
        body,
        name=name,
        out_shape=outs,
        in_specs=[s for _, s in pairs],
        out_specs=jax.tree.map(lambda _: VMEM, outs),
        scratch_shapes=list(scratch),
        cost_estimate=pl.CostEstimate(flops=flops, bytes_accessed=moved, transcendentals=0),
        compiler_params=pltpu.CompilerParams(vmem_limit_bytes=16 << 20),
    )(*[a for a, _ in pairs])


def stencil(pick):
    summed = None
    for k in range(1, 5):
        term = COEF[k - 1] * (pick(k) - pick(-k))
        summed = term if summed is None else summed + term
    return summed


def halves(tile):
    high = tile.astype(jnp.bfloat16)
    return high, (tile - high.astype(jnp.float32)).astype(jnp.bfloat16)


def diff_z(tile, matrix):
    return jnp.dot(
        jnp.concatenate(halves(tile), axis=1), matrix[...], preferred_element_type=jnp.float32
    )


def diff_y(tile, matrix):
    return jnp.dot(
        matrix[...], jnp.concatenate(halves(tile), axis=0), preferred_element_type=jnp.float32
    )


def diff_matrix(size, along, shape):
    row = lax.broadcasted_iota(jnp.int32, shape, 0) % size
    column = lax.broadcasted_iota(jnp.int32, shape, 1) % size
    offset = row - column if along == 0 else column - row
    entries = jnp.zeros(shape, jnp.float32)
    for k in range(1, 5):
        entries = jnp.where(offset == k, WHOLE[k - 1], entries)
        entries = jnp.where(offset == -k, -WHOLE[k - 1], entries)
    return entries.astype(jnp.bfloat16)


def place_halos(wide, own, partner, across):
    rows, halo = own.shape[0], sum(ref.shape[0] for ref in partner)
    blk, blocks = lax.axis_index("blk"), lax.axis_size("blk")
    odd = blk % 2
    outside = (blk == 0) | (blk == blocks - 1)
    above = halo + rows
    wide[halo:above] = own[...]
    partner_at = jnp.where(odd == 1, 0, above)
    across_at = jnp.where(odd == 1, above, 0)
    for ref_p, ref_a in zip(partner, across):
        part = ref_p.shape[0]
        wide[pl.ds(partner_at, part)] = ref_p[...]
        wide[pl.ds(across_at, part)] = jnp.where(outside, 0.0, ref_a[...])
        partner_at, across_at = partner_at + part, across_at + part


def slopes_yz(wide, first, out_y, out_z, matrix_y, matrix_z):
    for i in range(out_z.shape[0]):
        out_z[i] = diff_z(wide[first + i] * UNIT, matrix_z)
    for i in range(out_y.shape[0]):
        out_y[i] = diff_y(wide[first + i] * UNIT, matrix_y)


def apply_operator(halos, coef, matrix_y, matrix_z, scratch, finish):
    wide, flux_x, all_y, all_z, part = scratch
    rows = part.shape[0]
    own, partner, across = halos
    place_halos(wide, own, (partner,), (across,))
    slopes_yz(wide, 4, all_y, all_z, matrix_y, matrix_z)
    for i in range(rows + 8):
        slope_x = stencil(lambda k: wide[i + 4 + k])
        slope_y, slope_z = all_y[i], all_z[i]
        along = coef[0, i] * slope_x + coef[1, i] * slope_y + coef[2, i] * slope_z
        flux_x[i] = coef[3, i] * slope_x - coef[0, i] * along
        if 4 <= i < rows + 4:
            part[i - 4] = UNIT * (
                diff_z(coef[3, i] * slope_z - coef[2, i] * along, matrix_z)
                + diff_y(coef[3, i] * slope_y - coef[1, i] * along, matrix_y)
            )
    for r in range(rows):
        finish(r, stencil(lambda k: flux_x[r + 4 + k]) + part[r])


def sin_cos(angle):
    square = angle * angle
    sine, cosine = 0.0, 1.0 / 479001600.0
    for factor in (-39916800.0, 362880.0, -5040.0, 120.0, -6.0, 1.0):
        sine = sine * square + 1.0 / factor
    for factor in (-3628800.0, 40320.0, -720.0, 24.0, -2.0, 1.0):
        cosine = cosine * square + 1.0 / factor
    return angle * sine, cosine


def owner_kernel(eps, tilt, azimuth, speed, state, wx, wy, wz, out, current, held, sems):
    rows = wx.shape[0]
    copies = [
        pltpu.make_async_copy(ref, to, sems.at[n])
        for n, (ref, to) in enumerate(
            (
                (eps, held.at[0]),
                (tilt, held.at[1]),
                (azimuth, held.at[2]),
                (speed, out),
                (state.at[0], current),
            )
        )
    ]
    for copy in copies:
        copy.start()
    for copy in copies[:3]:
        copy.wait()
    for r in range(rows):
        size = jnp.sqrt(2.0 * held[0, r])
        sin_tilt, cos_tilt = sin_cos(held[1, r])
        sin_half, cos_half = sin_cos(0.5 * held[2, r])
        flat = size * sin_tilt
        wx[r] = flat * (1.0 - 2.0 * sin_half * sin_half)
        wy[r] = flat * (2.0 * sin_half * cos_half)
        wz[r] = size * cos_tilt
    for copy in copies[3:]:
        copy.wait()


def first_kernel(anchor, wz, first, wz_first):
    rows, count, depth = wz.shape
    number = (anchor[...].reshape(1, 1) // count).astype(jnp.float32)
    number = jnp.broadcast_to(number, (count, depth))
    first[...] = number[0:8]
    wz_first[0:rows] = wz[...]
    wz_first[rows] = number


def prepare_kernel(shots, parts, first, own, partner, across, *refs):
    slope, flags, matrix_y, matrix_z, wide = refs[-5:]
    rows, width, depth = own.shape
    matrix_y[...] = diff_matrix(width, 1, matrix_y.shape)
    matrix_z[...] = diff_matrix(depth, 0, matrix_z.shape)
    me = lax.axis_index("shot")
    for k in range(shots):
        part = jnp.bitwise_xor(me, k).astype(jnp.float32) - first[0:1, :]
        for j in range(parts):
            flags[k * parts + j : k * parts + j + 1, :] = jnp.where(
                jnp.abs(part - j) < 0.5, 1.0, 0.0
            )
    place_halos(wide, own, (partner,), (across,))
    slopes_yz(wide, 4, slope.at[1], slope.at[2], matrix_y, matrix_z)
    for i in range(rows + 8):
        slope[0, i] = stencil(lambda k: wide[i + 4 + k])


def inject_kernel(step, sx, sy, sz, wavelet, rx, ry, rz, traces, src, inj):
    rows, width, depth = src.shape[1:]
    start, sx, sy, sz = (ref[...].reshape(1, 1) for ref in (step, sx, sy, sz))
    first = lax.axis_index("blk") * rows
    shape = (rows, width, depth)
    plane = (width, depth)
    here = (lax.broadcasted_iota(jnp.int32, plane, 0) == sy) & (
        lax.broadcasted_iota(jnp.int32, plane, 1) == sz
    )
    moment = lax.broadcasted_iota(jnp.int32, wavelet.shape, 1)
    for t in range(STEPS - 1):
        chosen = jnp.where(moment == start + t, wavelet[...], 0.0)
        value = jnp.sum(chosen, axis=1, keepdims=True)
        for r in range(rows):
            src[t, r] = jnp.where(here & (sx == first + r), value, 0.0)
    receivers = rx.shape[1]
    local = rx[...] - first
    cell = jnp.where((local >= 0) & (local < rows), local * width + ry[...], -1)
    pick = (
        lax.broadcasted_iota(jnp.int32, (rows * width, receivers), 0) == cell
    ).astype(jnp.float32)
    match = lax.broadcasted_iota(jnp.int32, (depth, receivers), 0) == rz[...]
    moment = lax.broadcasted_iota(jnp.int32, traces.shape[1:], 0)
    for t in range(STEPS):
        chosen = jnp.where(moment == start + t, traces[0], 0.0)
        samples = jnp.sum(chosen, axis=0, keepdims=True)
        spread = jnp.where(match, samples, 0.0)
        added = lax.dot_general(
            pick,
            spread,
            (((1,), (1,)), ((), ())),
            precision=lax.Precision.HIGHEST,
            preferred_element_type=jnp.float32,
        )
        inj[t] = added.reshape(shape)


def relay_kernel(parts, wz_first, own, received, *refs):
    out = refs[-1]
    first = wz_first[wz_first.shape[0] - 1, 0:1, :]
    part = lax.axis_index("shot").astype(jnp.float32) - first
    inside = (part > -0.5) & (part < parts - 0.5)
    out[...] = jnp.where(inside, own[...], received[...])


def pair_kernel(own, received, out):
    out[0] = own[...]
    out[1] = received[0 : own.shape[0]]


def window_part(pieces, flags, parts, j):
    chosen = pieces[-1][...]
    for k in reversed(range(len(pieces) - 1)):
        at = k * parts + j
        chosen = jnp.where(flags[at : at + 1, :] > 0.5, pieces[k][...], chosen)
    return chosen


def piece_refs(refs, places):
    return [refs[i] if at is None else refs[i].at[at] for i, at in places]


def flux_kernel(places, parts, flags, slope, matrix_y, matrix_z, *refs):
    tensor, flux, rest, edge_a0, edge_a1, edge_p0, edge_p1 = refs[-7:]
    rows, width, _ = flux.shape
    count = width // parts
    for a in range(3):
        pieces = piece_refs(refs, places[a])
        for j in range(parts):
            tensor[a, :, j * count : (j + 1) * count, :] = window_part(pieces, flags, parts, j)
    odd = lax.axis_index("blk") % 2
    low = rows - 4
    for n, (out_a, out_p) in enumerate(((edge_a0, edge_p0), (edge_a1, edge_p1))):
        out_a[...] = tensor[:, pl.ds(odd * low + 2 * n, 2)]
        out_p[...] = tensor[:, pl.ds((1 - odd) * low + 2 * n, 2)]
    for r in range(rows):
        wx, wy, wz = tensor[0, r], tensor[1, r], tensor[2, r]
        along = wx * slope[0, r + 4] + wy * slope[1, r + 4] + wz * slope[2, r + 4]
        size = 1.0 + (wx * wx + wy * wy + wz * wz)
        flux[r] = size * slope[0, r + 4] - wx * along
        rest[r] = UNIT * (
            diff_z(size * slope[2, r + 4] - wz * along, matrix_z)
            + diff_y(size * slope[1, r + 4] - wy * along, matrix_y)
        )


def speed_kernel(places, parts, flags, present, *refs):
    speed, operand = refs[-2:]
    pieces = piece_refs(refs, places)
    count = speed.shape[1] // parts
    for j in range(parts):
        speed[:, j * count : (j + 1) * count, :] = window_part(pieces, flags, parts, j)
    operand[...] = speed[...] * present[...]


def forward_first(tensor, edge_p0, edge_p1, edge_a0, edge_a1, slope, flux, rest, own, previous, speed, src,
                  image, following, coef, flux_x):
    rows = rest.shape[0]
    blk, blocks = lax.axis_index("blk"), lax.axis_size("blk")
    for a in range(3):
        place_halos(coef.at[a], tensor.at[a], (edge_p0.at[a], edge_p1.at[a]),
                    (edge_a0.at[a], edge_a1.at[a]))
    for i in range(rows + 8):
        wx, wy, wz = coef[0, i], coef[1, i], coef[2, i]
        size = 1.0 + (wx * wx + wy * wy + wz * wz)
        if i < 4:
            size = jnp.where(blk == 0, 0.0, size)
        if i >= rows + 4:
            size = jnp.where(blk == blocks - 1, 0.0, size)
        coef[3, i] = size
        if 4 <= i < rows + 4:
            flux_x[i] = flux[i - 4]
        else:
            along = wx * slope[0, i] + wy * slope[1, i] + wz * slope[2, i]
            flux_x[i] = size * slope[0, i] - wx * along
    for r in range(rows):
        value = stencil(lambda k: flux_x[r + 4 + k]) + rest[r]
        image[r] = value
        following[r] = 2.0 * own[r] - previous[r] + speed[r] * value + src[0, r]


def forward(t, own, across, partner, coef, matrix_y, matrix_z, previous, speed, src,
            image, following, *scratch):
    def finish(r, value):
        image[r] = value
        following[r] = 2.0 * own[r] - previous[r] + speed[r] * value + src[t, r]

    apply_operator((own, partner, across), coef, matrix_y, matrix_z, scratch, finish)


def backward(t, own, across, partner, coef, matrix_y, matrix_z, present, later, inj, *refs):
    refs, scratch = refs[:-5], refs[-5:]
    if t == 0:
        earlier, copied, done = refs
        copied[...] = present[...]
        done[...] = jnp.zeros(done.shape, jnp.float32)
    elif t == 1:
        speed, lambda3, image0, image1, image2, earlier, operand, known = refs
    else:
        speed, earlier, operand = refs

    def finish(r, value):
        result = 2.0 * present[r] - later[r] + value + inj[t, r]
        earlier[r] = result
        if t > 0:
            operand[r] = speed[r] * result
        if t == 1:
            known[r] = lambda3[r] * image2[r] + present[r] * image1[r] + result * image0[r]

    apply_operator((own, partner, across), coef, matrix_y, matrix_z, scratch, finish)


def forward_last(parts, own, across, partner, coef, matrix_y, matrix_z, known, lambda4, flags,
                 *refs):
    chunks, scratch, grad = refs[:-6], refs[-6:-1], refs[-1]
    count = chunks[0].shape[1]

    def finish(r, value):
        grad[r] = known[r] + lambda4[r] * value

    apply_operator((own, partner, across), coef, matrix_y, matrix_z, scratch, finish)
    for k, chunk in enumerate(chunks):
        held = jnp.zeros(chunk.shape, jnp.float32)
        for j in range(parts):
            at = k * parts + j
            held = jnp.where(
                flags[at : at + 1, :] > 0.5, grad[:, j * count : (j + 1) * count, :], held
            )
        chunk[...] = held


def total_kernel(*refs):
    out = refs[-1]
    total = refs[0][...]
    for ref in refs[1:-2]:
        total = total + ref[...]
    out[...] = total


def on_device(
    state_before,
    state_now,
    adjoint_later,
    adjoint_now,
    courant_sq,
    epsilon,
    tilt_angle,
    azimuth,
    aperture_anchor,
    step_index,
    wavelet,
    residual_traces,
    source_x,
    source_y,
    source_z,
    receiver_x,
    receiver_y,
    receiver_z,
):
    rows, width, depth = state_now.shape[1:]
    count = courant_sq.shape[1]
    parts = width // count
    shots = lax.axis_size("shot")
    blocks = lax.axis_size("blk")
    field, piece = f32(rows, width, depth), f32(rows, count, depth)
    extended = pltpu.VMEM((rows + 8, width, depth), jnp.float32)
    wide = pltpu.VMEM((3 * rows, width, depth), jnp.float32)
    own_rows = pltpu.VMEM((rows, width, depth), jnp.float32)
    scratch = (wide, extended, extended, extended, own_rows)
    work = 100 * (rows + 8) * width * depth

    core_pairs = [(i, i ^ 1) for i in range(blocks)]
    def chip_pairs(hop):
        pairs = []
        for s in range(shots):
            for b in range(blocks):
                end = b in (0, blocks - 1)
                other = (s ^ hop, b) if end else (s, b - 1 + 2 * (b % 2))
                pairs.append((s * blocks + b, other[0] * blocks + other[1]))
        return pairs

    def to_partner(array, name):
        with jax.named_scope(f"{name}_to_core"):
            return lax.ppermute(array, "blk", core_pairs)

    def across_chips(array, name, hop=2):
        with jax.named_scope(f"{name}_to_chip"):
            return lax.ppermute(array, ("shot", "blk"), chip_pairs(hop))

    def halos(array, name):
        return to_partner(array, name), across_chips(array, name)

    def in_hbm(array):
        return pltpu.with_memory_space_constraint(array, pltpu.HBM), HBM

    def to_owners(array, k, name):
        with jax.named_scope(f"{name}_to_{k}"):
            return lax.ppermute(array, "shot", [(i, i ^ k) for i in range(shots)])

    previous = state_before[0]
    present, later = adjoint_now[0], adjoint_later[0]

    wx, wy, wz, speed, current = call(
        "owner",
        owner_kernel,
        (piece,) * 4 + (field,),
        [in_hbm(a) for a in (epsilon, tilt_angle, azimuth, courant_sq, state_now)],
        (
            pltpu.VMEM((3, rows, count, depth), jnp.float32),
            pltpu.SemaphoreType.DMA((5,)),
        ),
    )
    first, wz_first = call(
        "first",
        first_kernel,
        (f32(8, depth), f32(rows + 1, count, depth)),
        [aperture_anchor, wz],
    )

    if shots == 4 and parts == 2:
        relay = functools.partial(relay_kernel, parts)
        wx_y = to_owners(wx, 2, "wx")
        wz_x = to_owners(wz_first, 1, "wz")
        wy_y = to_owners(wy, 2, "wy")
        wx_sent = call("relay_wx", relay, piece, [wz_x, wx, wx_y])
        wx_x = to_owners(wx_sent, 1, "wx")
        both = f32(2, rows, count, depth)
        wz_y = to_owners(call("pair_wz", pair_kernel, both, [wz, wz_x]), 2, "wz")
        wy_sent = call("relay_wy", relay, piece, [wz_x, wy, wy_y, wx_sent])
        wy_x = to_owners(wy_sent, 1, "wy")
        speed_x = to_owners(speed, 1, "speed")
        speed_y = to_owners(call("pair_speed", pair_kernel, both, [speed, speed_x]), 2, "speed")
        before = [wx_x, speed_x]
        pieces = [wx, wx_x, wx_y, wy, wy_x, wy_y, wz, wz_x, wz_y]
        places = [
            [(0, None), (1, None), (2, None), (1, None)],
            [(3, None), (4, None), (5, None), (4, None)],
            [(6, None), (7, slice(0, rows)), (8, 0), (8, 1)],
        ]
        speed_pieces = [speed, speed_x, speed_y]
        speed_places = [(0, None), (1, None), (2, 0), (2, 1)]
    else:
        pieces, places, before = [], [], []
        for array in (wx, wy, wz):
            places.append([(len(pieces) + k, None) for k in range(shots)])
            pieces = pieces + [array] + [to_owners(array, k, "w") for k in range(1, shots)]
        speed_places = places[0]
        speed_pieces = [speed] + [to_owners(speed, k, "speed") for k in range(1, shots)]

    now_p, now_a = to_partner(current, "state"), across_chips(current, "state", 1)
    slope, flags, matrix_y, matrix_z = call(
        "prepare",
        functools.partial(prepare_kernel, shots, parts),
        (
            f32(3, rows + 8, width, depth),
            f32(shots * parts, depth),
            jax.ShapeDtypeStruct((width, 2 * width), jnp.bfloat16),
            jax.ShapeDtypeStruct((2 * depth, depth), jnp.bfloat16),
        ),
        [first, current, now_p, now_a] + before,
        [wide],
    )
    edge = f32(3, 2, width, depth)
    tensor, flux, rest, *edges = call(
        "flux",
        functools.partial(flux_kernel, places, parts),
        (f32(3, rows, width, depth), field, field) + (edge,) * 4,
        [flags, slope, matrix_y, matrix_z] + pieces,
        flops=work // 3,
    )
    edges_a = [across_chips(a, "edge") for a in edges[:2]]
    edges_p = [to_partner(a, "edge") for a in edges[2:]]
    src, inj = call(
        "inject",
        inject_kernel,
        (f32(STEPS - 1, rows, width, depth), f32(STEPS, rows, width, depth)),
        [step_index, source_x, source_y, source_z, wavelet, receiver_x, receiver_y, receiver_z]
        + [residual_traces],
    )

    speed, operand = call(
        "speed",
        functools.partial(speed_kernel, speed_places, parts),
        (field, field),
        [flags, present] + speed_pieces,
    )
    op_p, op_a = halos(operand, "adjoint")

    image, following, coef = call(
        "forward0",
        forward_first,
        (field, field, f32(4, rows + 8, width, depth)),
        [tensor, *edges_p, *edges_a, slope, flux, rest]
        + [current, previous, speed, src],
        [extended],
        work // 4,
    )
    images = [image]
    previous, current = current, following
    adjoints = [present]
    known = None
    for t in range(STEPS - 1):
        now_p, now_a = halos(current, "state")
        back = STEPS - 1 - t
        ins = [operand, op_a, op_p, coef, matrix_y, matrix_z, present, later, inj, speed]
        outs = (field, field)
        if back == 1:
            ins = ins + [adjoints[1]] + images
            outs = (field, field, field)
        result = call(
            f"backward{t}", functools.partial(backward, back), outs, ins, scratch, work
        )
        later, present, operand = present, result[0], result[1]
        if back == 1:
            known = result[2]
        adjoints.append(present)
        op_p, op_a = halos(operand, "adjoint")
        if t < STEPS - 2:
            image, following = call(
                f"forward{t + 1}",
                functools.partial(forward, t + 1),
                (field, field),
                [current, now_a, now_p, coef, matrix_y, matrix_z, previous, speed, src],
                scratch,
                work,
            )
            images.append(image)
            previous, current = current, following

    chunks = call(
        "forward3",
        functools.partial(forward_last, parts),
        (piece,) * shots,
        [current, now_a, now_p, coef, matrix_y, matrix_z, known, adjoints[0], flags],
        scratch + (own_rows,),
        work,
    )
    received = [to_owners(chunks[k], k, "grad") for k in range(1, shots)]
    final, copied, done = call(
        "backward3",
        functools.partial(backward, 0),
        (field, field, f32(8, depth)),
        [operand, op_a, op_p, coef, matrix_y, matrix_z, present, later, inj],
        scratch,
        work,
    )
    model_grad = call("total", total_kernel, piece, [chunks[0]] + received + [done])
    return (copied[None], final[None], model_grad)


def solution(mesh):
    in_specs = (
        P("shot", "blk", None, None),
        P("shot", "blk", None, None),
        P("shot", "blk", None, None),
        P("shot", "blk", None, None),
        P("blk", "shot", None),
        P("blk", "shot", None),
        P("blk", "shot", None),
        P("blk", "shot", None),
        P("shot"),
        P(),
        P("shot", None),
        P("shot", None, None),
        P("shot"),
        P("shot"),
        P("shot"),
        P("shot", None),
        P("shot", None),
        P("shot", None),
    )
    out_specs = (P("shot", "blk", None, None), P("shot", "blk", None, None), P("blk", "shot", None))
    return jax.shard_map(
        on_device, mesh=mesh, in_specs=in_specs, out_specs=out_specs, check_vma=False
    )
```

```python
import functools

import jax
import jax.numpy as jnp
from jax import lax
from jax.experimental import pallas as pl
from jax.experimental.pallas import tpu as pltpu
from jax.sharding import PartitionSpec as P

STEPS = 4
COEF = (0.8, -0.2, 4.0 / 105.0, -1.0 / 280.0)
WHOLE = (672.0, -168.0, 32.0, -3.0)
UNIT = 1.0 / 840.0

VMEM = pl.BlockSpec(memory_space=pltpu.VMEM)
SMEM = pl.BlockSpec(memory_space=pltpu.SMEM)
HBM = pl.BlockSpec(memory_space=pltpu.HBM)


def f32(*shape):
    return jax.ShapeDtypeStruct(shape, jnp.float32)


def call(name, body, outs, ins, scratch=(), flops=1 << 20, moved=1 << 20):
    pairs = [a if isinstance(a, tuple) else (a, VMEM) for a in ins]
    return pl.pallas_call(
        body,
        name=name,
        out_shape=outs,
        in_specs=[s for _, s in pairs],
        out_specs=jax.tree.map(lambda _: VMEM, outs),
        scratch_shapes=list(scratch),
        cost_estimate=pl.CostEstimate(flops=flops, bytes_accessed=moved, transcendentals=0),
        compiler_params=pltpu.CompilerParams(vmem_limit_bytes=16 << 20),
    )(*[a for a, _ in pairs])


def stencil(pick):
    summed = None
    for k in range(1, 5):
        term = COEF[k - 1] * (pick(k) - pick(-k))
        summed = term if summed is None else summed + term
    return summed


def halves(tile):
    high = tile.astype(jnp.bfloat16)
    return high, (tile - high.astype(jnp.float32)).astype(jnp.bfloat16)


def diff_z(tile, matrix):
    return jnp.dot(
        jnp.concatenate(halves(tile), axis=1), matrix[...], preferred_element_type=jnp.float32
    )


def diff_y(tile, matrix):
    return jnp.dot(
        matrix[...], jnp.concatenate(halves(tile), axis=0), preferred_element_type=jnp.float32
    )


def diff_matrix(size, along, shape):
    row = lax.broadcasted_iota(jnp.int32, shape, 0) % size
    column = lax.broadcasted_iota(jnp.int32, shape, 1) % size
    offset = row - column if along == 0 else column - row
    entries = jnp.zeros(shape, jnp.float32)
    for k in range(1, 5):
        entries = jnp.where(offset == k, WHOLE[k - 1], entries)
        entries = jnp.where(offset == -k, -WHOLE[k - 1], entries)
    return entries.astype(jnp.bfloat16)


def place_halos(wide, own, partner, across):
    rows, halo = own.shape[0], sum(ref.shape[0] for ref in partner)
    blk, blocks = lax.axis_index("blk"), lax.axis_size("blk")
    odd = blk % 2
    outside = (blk == 0) | (blk == blocks - 1)
    above = halo + rows
    wide[halo:above] = own[...]
    partner_at = jnp.where(odd == 1, 0, above)
    across_at = jnp.where(odd == 1, above, 0)
    for ref_p, ref_a in zip(partner, across):
        part = ref_p.shape[0]
        wide[pl.ds(partner_at, part)] = ref_p[...]
        wide[pl.ds(across_at, part)] = jnp.where(outside, 0.0, ref_a[...])
        partner_at, across_at = partner_at + part, across_at + part


def slopes_yz(wide, first, out_y, out_z, matrix_y, matrix_z):
    for i in range(out_z.shape[0]):
        out_z[i] = diff_z(wide[first + i] * UNIT, matrix_z)
    for i in range(out_y.shape[0]):
        out_y[i] = diff_y(wide[first + i] * UNIT, matrix_y)


def apply_operator(halos, coef, matrix_y, matrix_z, scratch, finish):
    wide, flux_x, all_y, all_z, part = scratch
    rows = part.shape[0]
    own, partner, across = halos
    place_halos(wide, own, (partner,), (across,))
    slopes_yz(wide, 4, all_y, all_z, matrix_y, matrix_z)
    for i in range(rows + 8):
        slope_x = stencil(lambda k: wide[i + 4 + k])
        slope_y, slope_z = all_y[i], all_z[i]
        along = coef[0, i] * slope_x + coef[1, i] * slope_y + coef[2, i] * slope_z
        flux_x[i] = coef[3, i] * slope_x - coef[0, i] * along
        if 4 <= i < rows + 4:
            part[i - 4] = UNIT * (
                diff_z(coef[3, i] * slope_z - coef[2, i] * along, matrix_z)
                + diff_y(coef[3, i] * slope_y - coef[1, i] * along, matrix_y)
            )
    for r in range(rows):
        finish(r, stencil(lambda k: flux_x[r + 4 + k]) + part[r])


def sin_cos(angle):
    square = angle * angle
    sine, cosine = 0.0, 1.0 / 479001600.0
    for factor in (-39916800.0, 362880.0, -5040.0, 120.0, -6.0, 1.0):
        sine = sine * square + 1.0 / factor
    for factor in (-3628800.0, 40320.0, -720.0, 24.0, -2.0, 1.0):
        cosine = cosine * square + 1.0 / factor
    return angle * sine, cosine


def owner_kernel(eps, tilt, azimuth, speed, state, wx, wy, wz, out, current, held, sems):
    rows = wx.shape[0]
    copies = [
        pltpu.make_async_copy(ref, to, sems.at[n])
        for n, (ref, to) in enumerate(
            (
                (eps, held.at[0]),
                (tilt, held.at[1]),
                (azimuth, held.at[2]),
                (speed, out),
                (state.at[0], current),
            )
        )
    ]
    for copy in copies:
        copy.start()
    for copy in copies[:3]:
        copy.wait()
    for r in range(rows):
        size = jnp.sqrt(2.0 * held[0, r])
        sin_tilt, cos_tilt = sin_cos(held[1, r])
        sin_half, cos_half = sin_cos(0.5 * held[2, r])
        flat = size * sin_tilt
        wx[r] = flat * (1.0 - 2.0 * sin_half * sin_half)
        wy[r] = flat * (2.0 * sin_half * cos_half)
        wz[r] = size * cos_tilt
    for copy in copies[3:]:
        copy.wait()


def first_kernel(anchor, wz, first, wz_first):
    rows, count, depth = wz.shape
    number = (anchor[...].reshape(1, 1) // count).astype(jnp.float32)
    number = jnp.broadcast_to(number, (count, depth))
    first[...] = number[0:8]
    wz_first[0:rows] = wz[...]
    wz_first[rows] = number


def prepare_kernel(shots, parts, first, own, partner, across, *refs):
    slope, flags, matrix_y, matrix_z, wide = refs[-5:]
    rows, width, depth = own.shape
    matrix_y[...] = diff_matrix(width, 1, matrix_y.shape)
    matrix_z[...] = diff_matrix(depth, 0, matrix_z.shape)
    me = lax.axis_index("shot")
    for k in range(shots):
        part = jnp.bitwise_xor(me, k).astype(jnp.float32) - first[0:1, :]
        for j in range(parts):
            flags[k * parts + j : k * parts + j + 1, :] = jnp.where(
                jnp.abs(part - j) < 0.5, 1.0, 0.0
            )
    place_halos(wide, own, (partner,), (across,))
    slopes_yz(wide, 4, slope.at[1], slope.at[2], matrix_y, matrix_z)
    for i in range(rows + 8):
        slope[0, i] = stencil(lambda k: wide[i + 4 + k])


def source_kernel(step, sx, sy, sz, wavelet, src):
    rows, width, depth = src.shape[1:]
    start, sx, sy, sz = (ref[...].reshape(1, 1) for ref in (step, sx, sy, sz))
    first = lax.axis_index("blk") * rows
    plane = (width, depth)
    here = (lax.broadcasted_iota(jnp.int32, plane, 0) == sy) & (
        lax.broadcasted_iota(jnp.int32, plane, 1) == sz
    )
    moment = lax.broadcasted_iota(jnp.int32, wavelet.shape, 1)
    for t in range(STEPS - 1):
        chosen = jnp.where(moment == start + t, wavelet[...], 0.0)
        value = jnp.sum(chosen, axis=1, keepdims=True)
        for r in range(rows):
            src[t, r] = jnp.where(here & (sx == first + r), value, 0.0)


def inject_kernel(step, rx, ry, rz, traces, inj):
    rows, width, depth = inj.shape[1:]
    start = step[...].reshape(1, 1)
    first = lax.axis_index("blk") * rows
    receivers = rx.shape[1]
    local = rx[...] - first
    cell = jnp.where((local >= 0) & (local < rows), local * width + ry[...], -1)
    pick = (
        lax.broadcasted_iota(jnp.int32, (rows * width, receivers), 0) == cell
    ).astype(jnp.float32)
    match = lax.broadcasted_iota(jnp.int32, (depth, receivers), 0) == rz[...]
    moment = lax.broadcasted_iota(jnp.int32, traces.shape[1:], 0)
    for t in range(STEPS):
        chosen = jnp.where(moment == start + t, traces[0], 0.0)
        samples = jnp.sum(chosen, axis=0, keepdims=True)
        spread = jnp.where(match, samples, 0.0)
        added = lax.dot_general(
            pick,
            spread,
            (((1,), (1,)), ((), ())),
            precision=lax.Precision.HIGHEST,
            preferred_element_type=jnp.float32,
        )
        inj[t] = added.reshape(rows, width, depth)


def relay_kernel(parts, wz_first, own, received, *refs):
    out = refs[-1]
    first = wz_first[wz_first.shape[0] - 1, 0:1, :]
    part = lax.axis_index("shot").astype(jnp.float32) - first
    inside = (part > -0.5) & (part < parts - 0.5)
    out[...] = jnp.where(inside, own[...], received[...])


def pair_kernel(own, received, out):
    out[0] = own[...]
    out[1] = received[0 : own.shape[0]]


def window_part(pieces, flags, parts, j):
    chosen = pieces[-1][...]
    for k in reversed(range(len(pieces) - 1)):
        at = k * parts + j
        chosen = jnp.where(flags[at : at + 1, :] > 0.5, pieces[k][...], chosen)
    return chosen


def piece_refs(refs, places):
    return [refs[i] if at is None else refs[i].at[at] for i, at in places]


def flux_kernel(places, parts, flags, slope, matrix_y, matrix_z, *refs):
    tensor, flux, rest, edge_a0, edge_a1, edge_p0, edge_p1 = refs[-7:]
    rows, width, _ = flux.shape
    count = width // parts
    for a in range(3):
        pieces = piece_refs(refs, places[a])
        for j in range(parts):
            tensor[a, :, j * count : (j + 1) * count, :] = window_part(pieces, flags, parts, j)
    odd = lax.axis_index("blk") % 2
    low = rows - 4
    for n, (out_a, out_p) in enumerate(((edge_a0, edge_p0), (edge_a1, edge_p1))):
        out_a[...] = tensor[:, pl.ds(odd * low + 2 * n, 2)]
        out_p[...] = tensor[:, pl.ds((1 - odd) * low + 2 * n, 2)]
    for r in range(rows):
        wx, wy, wz = tensor[0, r], tensor[1, r], tensor[2, r]
        along = wx * slope[0, r + 4] + wy * slope[1, r + 4] + wz * slope[2, r + 4]
        size = 1.0 + (wx * wx + wy * wy + wz * wz)
        flux[r] = size * slope[0, r + 4] - wx * along
        rest[r] = UNIT * (
            diff_z(size * slope[2, r + 4] - wz * along, matrix_z)
            + diff_y(size * slope[1, r + 4] - wy * along, matrix_y)
        )


def speed_kernel(places, parts, flags, present, *refs):
    speed, operand = refs[-2:]
    pieces = piece_refs(refs, places)
    count = speed.shape[1] // parts
    for j in range(parts):
        speed[:, j * count : (j + 1) * count, :] = window_part(pieces, flags, parts, j)
    operand[...] = speed[...] * present[...]


def forward_first(tensor, edge_p0, edge_p1, edge_a0, edge_a1, slope, flux, rest, own, previous, speed, src,
                  image, following, coef, flux_x):
    rows = rest.shape[0]
    blk, blocks = lax.axis_index("blk"), lax.axis_size("blk")
    for a in range(3):
        place_halos(coef.at[a], tensor.at[a], (edge_p0.at[a], edge_p1.at[a]),
                    (edge_a0.at[a], edge_a1.at[a]))
    for i in range(rows + 8):
        wx, wy, wz = coef[0, i], coef[1, i], coef[2, i]
        size = 1.0 + (wx * wx + wy * wy + wz * wz)
        if i < 4:
            size = jnp.where(blk == 0, 0.0, size)
        if i >= rows + 4:
            size = jnp.where(blk == blocks - 1, 0.0, size)
        coef[3, i] = size
        if 4 <= i < rows + 4:
            flux_x[i] = flux[i - 4]
        else:
            along = wx * slope[0, i] + wy * slope[1, i] + wz * slope[2, i]
            flux_x[i] = size * slope[0, i] - wx * along
    for r in range(rows):
        value = stencil(lambda k: flux_x[r + 4 + k]) + rest[r]
        image[r] = value
        following[r] = 2.0 * own[r] - previous[r] + speed[r] * value + src[0, r]


def forward(t, own, across, partner, coef, matrix_y, matrix_z, previous, speed, src,
            image, following, *scratch):
    def finish(r, value):
        image[r] = value
        following[r] = 2.0 * own[r] - previous[r] + speed[r] * value + src[t, r]

    apply_operator((own, partner, across), coef, matrix_y, matrix_z, scratch, finish)


def backward(t, own, across, partner, coef, matrix_y, matrix_z, present, later, inj, *refs):
    refs, scratch = refs[:-5], refs[-5:]
    if t == 0:
        earlier, copied, done = refs
        copied[...] = present[...]
        done[...] = jnp.zeros(done.shape, jnp.float32)
    elif t == 1:
        speed, lambda3, image0, image1, image2, earlier, operand, known = refs
    else:
        speed, earlier, operand = refs

    def finish(r, value):
        result = 2.0 * present[r] - later[r] + value + inj[t, r]
        earlier[r] = result
        if t > 0:
            operand[r] = speed[r] * result
        if t == 1:
            known[r] = lambda3[r] * image2[r] + present[r] * image1[r] + result * image0[r]

    apply_operator((own, partner, across), coef, matrix_y, matrix_z, scratch, finish)


def forward_last(parts, own, across, partner, coef, matrix_y, matrix_z, known, lambda4, flags,
                 *refs):
    chunks, scratch, grad = refs[:-6], refs[-6:-1], refs[-1]
    count = chunks[0].shape[1]

    def finish(r, value):
        grad[r] = known[r] + lambda4[r] * value

    apply_operator((own, partner, across), coef, matrix_y, matrix_z, scratch, finish)
    for k, chunk in enumerate(chunks):
        held = jnp.zeros(chunk.shape, jnp.float32)
        for j in range(parts):
            at = k * parts + j
            held = jnp.where(
                flags[at : at + 1, :] > 0.5, grad[:, j * count : (j + 1) * count, :], held
            )
        chunk[...] = held


def total_kernel(*refs):
    out = refs[-1]
    total = refs[0][...]
    for ref in refs[1:-2]:
        total = total + ref[...]
    out[...] = total


def on_device(
    state_before,
    state_now,
    adjoint_later,
    adjoint_now,
    courant_sq,
    epsilon,
    tilt_angle,
    azimuth,
    aperture_anchor,
    step_index,
    wavelet,
    residual_traces,
    source_x,
    source_y,
    source_z,
    receiver_x,
    receiver_y,
    receiver_z,
):
    rows, width, depth = state_now.shape[1:]
    count = courant_sq.shape[1]
    parts = width // count
    shots = lax.axis_size("shot")
    blocks = lax.axis_size("blk")
    field, piece = f32(rows, width, depth), f32(rows, count, depth)
    extended = pltpu.VMEM((rows + 8, width, depth), jnp.float32)
    wide = pltpu.VMEM((3 * rows, width, depth), jnp.float32)
    own_rows = pltpu.VMEM((rows, width, depth), jnp.float32)
    scratch = (wide, extended, extended, extended, own_rows)
    work = 100 * (rows + 8) * width * depth

    core_pairs = [(i, i ^ 1) for i in range(blocks)]
    def chip_pairs(hop):
        pairs = []
        for s in range(shots):
            for b in range(blocks):
                end = b in (0, blocks - 1)
                other = (s ^ hop, b) if end else (s, b - 1 + 2 * (b % 2))
                pairs.append((s * blocks + b, other[0] * blocks + other[1]))
        return pairs

    def to_partner(array, name):
        with jax.named_scope(f"{name}_to_core"):
            return lax.ppermute(array, "blk", core_pairs)

    def across_chips(array, name, hop=2):
        with jax.named_scope(f"{name}_to_chip"):
            return lax.ppermute(array, ("shot", "blk"), chip_pairs(hop))

    def halos(array, name):
        return to_partner(array, name), across_chips(array, name)

    def in_hbm(array):
        return pltpu.with_memory_space_constraint(array, pltpu.HBM), HBM

    def to_owners(array, k, name):
        with jax.named_scope(f"{name}_to_{k}"):
            return lax.ppermute(array, "shot", [(i, i ^ k) for i in range(shots)])

    previous = state_before[0]
    present, later = adjoint_now[0], adjoint_later[0]

    wx, wy, wz, speed, current = call(
        "owner",
        owner_kernel,
        (piece,) * 4 + (field,),
        [in_hbm(a) for a in (epsilon, tilt_angle, azimuth, courant_sq, state_now)],
        (
            pltpu.VMEM((3, rows, count, depth), jnp.float32),
            pltpu.SemaphoreType.DMA((5,)),
        ),
    )
    first, wz_first = call(
        "first",
        first_kernel,
        (f32(8, depth), f32(rows + 1, count, depth)),
        [aperture_anchor, wz],
    )

    if shots == 4 and parts == 2:
        relay = functools.partial(relay_kernel, parts)
        wx_y = to_owners(wx, 2, "wx")
        wz_x = to_owners(wz_first, 1, "wz")
        wy_y = to_owners(wy, 2, "wy")
        wx_sent = call("relay_wx", relay, piece, [wz_x, wx, wx_y])
        wx_x = to_owners(wx_sent, 1, "wx")
        both = f32(2, rows, count, depth)
        wz_y = to_owners(call("pair_wz", pair_kernel, both, [wz, wz_x]), 2, "wz")
        wy_sent = call("relay_wy", relay, piece, [wz_x, wy, wy_y, wx_sent])
        wy_x = to_owners(wy_sent, 1, "wy")
        speed_x = to_owners(speed, 1, "speed")
        speed_y = to_owners(call("pair_speed", pair_kernel, both, [speed, speed_x]), 2, "speed")
        before = [wx_x, speed_x]
        pieces = [wx, wx_x, wx_y, wy, wy_x, wy_y, wz, wz_x, wz_y]
        places = [
            [(0, None), (1, None), (2, None), (1, None)],
            [(3, None), (4, None), (5, None), (4, None)],
            [(6, None), (7, slice(0, rows)), (8, 0), (8, 1)],
        ]
        speed_pieces = [speed, speed_x, speed_y]
        speed_places = [(0, None), (1, None), (2, 0), (2, 1)]
    else:
        pieces, places, before = [], [], []
        for array in (wx, wy, wz):
            places.append([(len(pieces) + k, None) for k in range(shots)])
            pieces = pieces + [array] + [to_owners(array, k, "w") for k in range(1, shots)]
        speed_places = places[0]
        speed_pieces = [speed] + [to_owners(speed, k, "speed") for k in range(1, shots)]

    now_p, now_a = to_partner(current, "state"), across_chips(current, "state", 1)
    slope, flags, matrix_y, matrix_z = call(
        "prepare",
        functools.partial(prepare_kernel, shots, parts),
        (
            f32(3, rows + 8, width, depth),
            f32(shots * parts, depth),
            jax.ShapeDtypeStruct((width, 2 * width), jnp.bfloat16),
            jax.ShapeDtypeStruct((2 * depth, depth), jnp.bfloat16),
        ),
        [first, current, now_p, now_a] + before,
        [wide],
    )
    edge = f32(3, 2, width, depth)
    tensor, flux, rest, *edges = call(
        "flux",
        functools.partial(flux_kernel, places, parts),
        (f32(3, rows, width, depth), field, field) + (edge,) * 4,
        [flags, slope, matrix_y, matrix_z] + pieces,
        flops=work // 3,
    )
    edges_a = [across_chips(a, "edge") for a in edges[:2]]
    edges_p = [to_partner(a, "edge") for a in edges[2:]]
    src = call(
        "source",
        source_kernel,
        f32(STEPS - 1, rows, width, depth),
        [step_index, source_x, source_y, source_z, wavelet],
    )
    inj = call(
        "inject",
        inject_kernel,
        f32(STEPS, rows, width, depth),
        [step_index, receiver_x, receiver_y, receiver_z, residual_traces],
    )
    speed, operand = call(
        "speed",
        functools.partial(speed_kernel, speed_places, parts),
        (field, field),
        [flags, present] + speed_pieces,
    )
    op_p, op_a = halos(operand, "adjoint")

    image, following, coef = call(
        "forward0",
        forward_first,
        (field, field, f32(4, rows + 8, width, depth)),
        [tensor, *edges_p, *edges_a, slope, flux, rest]
        + [current, previous, speed, src],
        [extended],
        work // 4,
    )
    images = [image]
    previous, current = current, following
    adjoints = [present]
    known = None
    for t in range(STEPS - 1):
        now_p, now_a = halos(current, "state")
        back = STEPS - 1 - t
        ins = [operand, op_a, op_p, coef, matrix_y, matrix_z, present, later, inj, speed]
        outs = (field, field)
        if back == 1:
            ins = ins + [adjoints[1]] + images
            outs = (field, field, field)
        result = call(
            f"backward{t}", functools.partial(backward, back), outs, ins, scratch, work
        )
        later, present, operand = present, result[0], result[1]
        if back == 1:
            known = result[2]
        adjoints.append(present)
        op_p, op_a = halos(operand, "adjoint")
        if t < STEPS - 2:
            image, following = call(
                f"forward{t + 1}",
                functools.partial(forward, t + 1),
                (field, field),
                [current, now_a, now_p, coef, matrix_y, matrix_z, previous, speed, src],
                scratch,
                work,
            )
            images.append(image)
            previous, current = current, following

    chunks = call(
        "forward3",
        functools.partial(forward_last, parts),
        (piece,) * shots,
        [current, now_a, now_p, coef, matrix_y, matrix_z, known, adjoints[0], flags],
        scratch + (own_rows,),
        work,
    )
    received = [to_owners(chunks[k], k, "grad") for k in range(1, shots)]
    final, copied, done = call(
        "backward3",
        functools.partial(backward, 0),
        (field, field, f32(8, depth)),
        [operand, op_a, op_p, coef, matrix_y, matrix_z, present, later, inj],
        scratch,
        work,
    )
    model_grad = call("total", total_kernel, piece, [chunks[0]] + received + [done])
    return (copied[None], final[None], model_grad)


def solution(mesh):
    in_specs = (
        P("shot", "blk", None, None),
        P("shot", "blk", None, None),
        P("shot", "blk", None, None),
        P("shot", "blk", None, None),
        P("blk", "shot", None),
        P("blk", "shot", None),
        P("blk", "shot", None),
        P("blk", "shot", None),
        P("shot"),
        P(),
        P("shot", None),
        P("shot", None, None),
        P("shot"),
        P("shot"),
        P("shot"),
        P("shot", None),
        P("shot", None),
        P("shot", None),
    )
    out_specs = (P("shot", "blk", None, None), P("shot", "blk", None, None), P("blk", "shot", None))
    return jax.shard_map(
        on_device, mesh=mesh, in_specs=in_specs, out_specs=out_specs, check_vma=False
    )
```

```python
import functools

import jax
import jax.numpy as jnp
from jax import lax
from jax.experimental import pallas as pl
from jax.experimental.pallas import tpu as pltpu
from jax.sharding import PartitionSpec as P

STEPS = 4
COEF = (0.8, -0.2, 4.0 / 105.0, -1.0 / 280.0)
WHOLE = (672.0, -168.0, 32.0, -3.0)
UNIT = 1.0 / 840.0

VMEM = pl.BlockSpec(memory_space=pltpu.VMEM)
SMEM = pl.BlockSpec(memory_space=pltpu.SMEM)
HBM = pl.BlockSpec(memory_space=pltpu.HBM)


def f32(*shape):
    return jax.ShapeDtypeStruct(shape, jnp.float32)


def call(name, body, outs, ins, scratch=(), flops=1 << 20, moved=1 << 20):
    pairs = [a if isinstance(a, tuple) else (a, VMEM) for a in ins]
    return pl.pallas_call(
        body,
        name=name,
        out_shape=outs,
        in_specs=[s for _, s in pairs],
        out_specs=jax.tree.map(lambda _: VMEM, outs),
        scratch_shapes=list(scratch),
        cost_estimate=pl.CostEstimate(flops=flops, bytes_accessed=moved, transcendentals=0),
        compiler_params=pltpu.CompilerParams(vmem_limit_bytes=16 << 20),
    )(*[a for a, _ in pairs])


def stencil(pick):
    summed = None
    for k in range(1, 5):
        term = COEF[k - 1] * (pick(k) - pick(-k))
        summed = term if summed is None else summed + term
    return summed


def halves(tile):
    high = tile.astype(jnp.bfloat16)
    return high, (tile - high.astype(jnp.float32)).astype(jnp.bfloat16)


def diff_z(tile, matrix):
    return jnp.dot(
        jnp.concatenate(halves(tile), axis=1), matrix[...], preferred_element_type=jnp.float32
    )


def diff_y(tile, matrix):
    return jnp.dot(
        matrix[...], jnp.concatenate(halves(tile), axis=0), preferred_element_type=jnp.float32
    )


def diff_matrix(size, along, shape):
    row = lax.broadcasted_iota(jnp.int32, shape, 0) % size
    column = lax.broadcasted_iota(jnp.int32, shape, 1) % size
    offset = row - column if along == 0 else column - row
    entries = jnp.zeros(shape, jnp.float32)
    for k in range(1, 5):
        entries = jnp.where(offset == k, WHOLE[k - 1], entries)
        entries = jnp.where(offset == -k, -WHOLE[k - 1], entries)
    return entries.astype(jnp.bfloat16)


def place_halos(wide, own, partner, across):
    rows, halo = own.shape[0], sum(ref.shape[0] for ref in partner)
    blk, blocks = lax.axis_index("blk"), lax.axis_size("blk")
    odd = blk % 2
    outside = (blk == 0) | (blk == blocks - 1)
    above = halo + rows
    wide[halo:above] = own[...]
    partner_at = jnp.where(odd == 1, 0, above)
    across_at = jnp.where(odd == 1, above, 0)
    for ref_p, ref_a in zip(partner, across):
        part = ref_p.shape[0]
        wide[pl.ds(partner_at, part)] = ref_p[...]
        wide[pl.ds(across_at, part)] = jnp.where(outside, 0.0, ref_a[...])
        partner_at, across_at = partner_at + part, across_at + part


def slopes_yz(wide, first, out_y, out_z, matrix_y, matrix_z):
    for i in range(out_z.shape[0]):
        out_z[i] = diff_z(wide[first + i] * UNIT, matrix_z)
    for i in range(out_y.shape[0]):
        out_y[i] = diff_y(wide[first + i] * UNIT, matrix_y)


def apply_operator(halos, coef, matrix_y, matrix_z, scratch, finish):
    wide, flux_x, all_y, all_z, part = scratch
    rows = part.shape[0]
    own, partner, across = halos
    place_halos(wide, own, (partner,), (across,))
    slopes_yz(wide, 4, all_y, all_z, matrix_y, matrix_z)
    for i in range(rows + 8):
        slope_x = stencil(lambda k: wide[i + 4 + k])
        slope_y, slope_z = all_y[i], all_z[i]
        along = coef[0, i] * slope_x + coef[1, i] * slope_y + coef[2, i] * slope_z
        flux_x[i] = coef[3, i] * slope_x - coef[0, i] * along
        if 4 <= i < rows + 4:
            part[i - 4] = UNIT * (
                diff_z(coef[3, i] * slope_z - coef[2, i] * along, matrix_z)
                + diff_y(coef[3, i] * slope_y - coef[1, i] * along, matrix_y)
            )
    for r in range(rows):
        finish(r, stencil(lambda k: flux_x[r + 4 + k]) + part[r])


def sin_cos(angle):
    square = angle * angle
    sine, cosine = 0.0, 1.0 / 479001600.0
    for factor in (-39916800.0, 362880.0, -5040.0, 120.0, -6.0, 1.0):
        sine = sine * square + 1.0 / factor
    for factor in (-3628800.0, 40320.0, -720.0, 24.0, -2.0, 1.0):
        cosine = cosine * square + 1.0 / factor
    return angle * sine, cosine


def owner_kernel(eps, tilt, azimuth, speed, state, wx, wy, wz, out, current, held, sems):
    rows = wx.shape[0]
    copies = [
        pltpu.make_async_copy(ref, to, sems.at[n])
        for n, (ref, to) in enumerate(
            (
                (eps, held.at[0]),
                (tilt, held.at[1]),
                (azimuth, held.at[2]),
                (speed, out),
                (state.at[0], current),
            )
        )
    ]
    for copy in copies:
        copy.start()
    for copy in copies[:3]:
        copy.wait()
    for r in range(rows):
        size = jnp.sqrt(2.0 * held[0, r])
        sin_tilt, cos_tilt = sin_cos(held[1, r])
        sin_half, cos_half = sin_cos(0.5 * held[2, r])
        flat = size * sin_tilt
        wx[r] = flat * (1.0 - 2.0 * sin_half * sin_half)
        wy[r] = flat * (2.0 * sin_half * cos_half)
        wz[r] = size * cos_tilt
    for copy in copies[3:]:
        copy.wait()


def first_kernel(anchor, wz, first, wz_first):
    rows, count, depth = wz.shape
    number = (anchor[...].reshape(1, 1) // count).astype(jnp.float32)
    number = jnp.broadcast_to(number, (count, depth))
    first[...] = number[0:8]
    wz_first[0:rows] = wz[...]
    wz_first[rows] = number


def prepare_kernel(shots, parts, first, own, partner, across, *refs):
    slope, flags, matrix_y, matrix_z, wide = refs[-5:]
    rows, width, depth = own.shape
    matrix_y[...] = diff_matrix(width, 1, matrix_y.shape)
    matrix_z[...] = diff_matrix(depth, 0, matrix_z.shape)
    me = lax.axis_index("shot")
    for k in range(shots):
        part = jnp.bitwise_xor(me, k).astype(jnp.float32) - first[0:1, :]
        for j in range(parts):
            flags[k * parts + j : k * parts + j + 1, :] = jnp.where(
                jnp.abs(part - j) < 0.5, 1.0, 0.0
            )
    place_halos(wide, own, (partner,), (across,))
    slopes_yz(wide, 4, slope.at[1], slope.at[2], matrix_y, matrix_z)
    for i in range(rows + 8):
        slope[0, i] = stencil(lambda k: wide[i + 4 + k])


def inject_kernel(step, sx, sy, sz, wavelet, rx, ry, rz, traces, src, inj):
    rows, width, depth = src.shape[1:]
    start, sx, sy, sz = (ref[...].reshape(1, 1) for ref in (step, sx, sy, sz))
    first = lax.axis_index("blk") * rows
    shape = (rows, width, depth)
    plane = (width, depth)
    here = (lax.broadcasted_iota(jnp.int32, plane, 0) == sy) & (
        lax.broadcasted_iota(jnp.int32, plane, 1) == sz
    )
    moment = lax.broadcasted_iota(jnp.int32, wavelet.shape, 1)
    for t in range(STEPS - 1):
        chosen = jnp.where(moment == start + t, wavelet[...], 0.0)
        value = jnp.sum(chosen, axis=1, keepdims=True)
        for r in range(rows):
            src[t, r] = jnp.where(here & (sx == first + r), value, 0.0)
    receivers = rx.shape[1]
    local = rx[...] - first
    cell = jnp.where((local >= 0) & (local < rows), local * width + ry[...], -1)
    pick = (
        (lax.broadcasted_iota(jnp.int32, (rows * width, receivers), 0) == cell)
        .astype(jnp.float32)
        .astype(jnp.bfloat16)
    )
    pick = jnp.concatenate([pick, pick, pick], axis=1)
    match = lax.broadcasted_iota(jnp.int32, (depth, receivers), 0) == rz[...]
    moment = lax.broadcasted_iota(jnp.int32, traces.shape[1:], 0)
    for t in range(STEPS):
        chosen = jnp.where(moment == start + t, traces[0], 0.0)
        samples = jnp.sum(chosen, axis=0, keepdims=True)
        spread = jnp.where(match, samples, 0.0)
        high, low = halves(spread)
        middle, low = low, spread - high.astype(jnp.float32) - low.astype(jnp.float32)
        added = lax.dot_general(
            pick,
            jnp.concatenate([high, middle, low.astype(jnp.bfloat16)], axis=1),
            (((1,), (1,)), ((), ())),
            preferred_element_type=jnp.float32,
        )
        inj[t] = added.reshape(shape)


def relay_kernel(parts, wz_first, own, received, *refs):
    out = refs[-1]
    first = wz_first[wz_first.shape[0] - 1, 0:1, :]
    part = lax.axis_index("shot").astype(jnp.float32) - first
    inside = (part > -0.5) & (part < parts - 0.5)
    out[...] = jnp.where(inside, own[...], received[...])


def pair_kernel(own, received, out):
    out[0] = own[...]
    out[1] = received[0 : own.shape[0]]


def window_part(pieces, flags, parts, j):
    chosen = pieces[-1][...]
    for k in reversed(range(len(pieces) - 1)):
        at = k * parts + j
        chosen = jnp.where(flags[at : at + 1, :] > 0.5, pieces[k][...], chosen)
    return chosen


def piece_refs(refs, places):
    return [refs[i] if at is None else refs[i].at[at] for i, at in places]


def flux_kernel(places, parts, flags, slope, matrix_y, matrix_z, *refs):
    tensor, flux, rest, edge_a0, edge_a1, edge_p0, edge_p1 = refs[-7:]
    rows, width, _ = flux.shape
    count = width // parts
    for a in range(3):
        pieces = piece_refs(refs, places[a])
        for j in range(parts):
            tensor[a, :, j * count : (j + 1) * count, :] = window_part(pieces, flags, parts, j)
    odd = lax.axis_index("blk") % 2
    low = rows - 4
    for n, (out_a, out_p) in enumerate(((edge_a0, edge_p0), (edge_a1, edge_p1))):
        out_a[...] = tensor[:, pl.ds(odd * low + 2 * n, 2)]
        out_p[...] = tensor[:, pl.ds((1 - odd) * low + 2 * n, 2)]
    for r in range(rows):
        wx, wy, wz = tensor[0, r], tensor[1, r], tensor[2, r]
        along = wx * slope[0, r + 4] + wy * slope[1, r + 4] + wz * slope[2, r + 4]
        size = 1.0 + (wx * wx + wy * wy + wz * wz)
        flux[r] = size * slope[0, r + 4] - wx * along
        rest[r] = UNIT * (
            diff_z(size * slope[2, r + 4] - wz * along, matrix_z)
            + diff_y(size * slope[1, r + 4] - wy * along, matrix_y)
        )


def speed_kernel(places, parts, flags, present, *refs):
    speed, operand = refs[-2:]
    pieces = piece_refs(refs, places)
    count = speed.shape[1] // parts
    for j in range(parts):
        speed[:, j * count : (j + 1) * count, :] = window_part(pieces, flags, parts, j)
    operand[...] = speed[...] * present[...]


def forward_first(tensor, edge_p0, edge_p1, edge_a0, edge_a1, slope, flux, rest, own, previous, speed, src,
                  image, following, coef, flux_x):
    rows = rest.shape[0]
    blk, blocks = lax.axis_index("blk"), lax.axis_size("blk")
    for a in range(3):
        place_halos(coef.at[a], tensor.at[a], (edge_p0.at[a], edge_p1.at[a]),
                    (edge_a0.at[a], edge_a1.at[a]))
    for i in range(rows + 8):
        wx, wy, wz = coef[0, i], coef[1, i], coef[2, i]
        size = 1.0 + (wx * wx + wy * wy + wz * wz)
        if i < 4:
            size = jnp.where(blk == 0, 0.0, size)
        if i >= rows + 4:
            size = jnp.where(blk == blocks - 1, 0.0, size)
        coef[3, i] = size
        if 4 <= i < rows + 4:
            flux_x[i] = flux[i - 4]
        else:
            along = wx * slope[0, i] + wy * slope[1, i] + wz * slope[2, i]
            flux_x[i] = size * slope[0, i] - wx * along
    for r in range(rows):
        value = stencil(lambda k: flux_x[r + 4 + k]) + rest[r]
        image[r] = value
        following[r] = 2.0 * own[r] - previous[r] + speed[r] * value + src[0, r]


def forward(t, own, across, partner, coef, matrix_y, matrix_z, previous, speed, src,
            image, following, *scratch):
    def finish(r, value):
        image[r] = value
        following[r] = 2.0 * own[r] - previous[r] + speed[r] * value + src[t, r]

    apply_operator((own, partner, across), coef, matrix_y, matrix_z, scratch, finish)


def backward(t, own, across, partner, coef, matrix_y, matrix_z, present, later, inj, *refs):
    refs, scratch = refs[:-5], refs[-5:]
    if t == 0:
        earlier, copied, done = refs
        copied[...] = present[...]
        done[...] = jnp.zeros(done.shape, jnp.float32)
    elif t == 1:
        speed, lambda3, image0, image1, image2, earlier, operand, known = refs
    else:
        speed, earlier, operand = refs

    def finish(r, value):
        result = 2.0 * present[r] - later[r] + value + inj[t, r]
        earlier[r] = result
        if t > 0:
            operand[r] = speed[r] * result
        if t == 1:
            known[r] = lambda3[r] * image2[r] + present[r] * image1[r] + result * image0[r]

    apply_operator((own, partner, across), coef, matrix_y, matrix_z, scratch, finish)


def forward_last(parts, own, across, partner, coef, matrix_y, matrix_z, known, lambda4, flags,
                 *refs):
    chunks, scratch, grad = refs[:-6], refs[-6:-1], refs[-1]
    count = chunks[0].shape[1]

    def finish(r, value):
        grad[r] = known[r] + lambda4[r] * value

    apply_operator((own, partner, across), coef, matrix_y, matrix_z, scratch, finish)
    for k, chunk in enumerate(chunks):
        held = jnp.zeros(chunk.shape, jnp.float32)
        for j in range(parts):
            at = k * parts + j
            held = jnp.where(
                flags[at : at + 1, :] > 0.5, grad[:, j * count : (j + 1) * count, :], held
            )
        chunk[...] = held


def total_kernel(*refs):
    out = refs[-1]
    total = refs[0][...]
    for ref in refs[1:-2]:
        total = total + ref[...]
    out[...] = total


def on_device(
    state_before,
    state_now,
    adjoint_later,
    adjoint_now,
    courant_sq,
    epsilon,
    tilt_angle,
    azimuth,
    aperture_anchor,
    step_index,
    wavelet,
    residual_traces,
    source_x,
    source_y,
    source_z,
    receiver_x,
    receiver_y,
    receiver_z,
):
    rows, width, depth = state_now.shape[1:]
    count = courant_sq.shape[1]
    parts = width // count
    shots = lax.axis_size("shot")
    blocks = lax.axis_size("blk")
    field, piece = f32(rows, width, depth), f32(rows, count, depth)
    extended = pltpu.VMEM((rows + 8, width, depth), jnp.float32)
    wide = pltpu.VMEM((3 * rows, width, depth), jnp.float32)
    own_rows = pltpu.VMEM((rows, width, depth), jnp.float32)
    scratch = (wide, extended, extended, extended, own_rows)
    work = 100 * (rows + 8) * width * depth

    core_pairs = [(i, i ^ 1) for i in range(blocks)]
    def chip_pairs(hop):
        pairs = []
        for s in range(shots):
            for b in range(blocks):
                end = b in (0, blocks - 1)
                other = (s ^ hop, b) if end else (s, b - 1 + 2 * (b % 2))
                pairs.append((s * blocks + b, other[0] * blocks + other[1]))
        return pairs

    def to_partner(array, name):
        with jax.named_scope(f"{name}_to_core"):
            return lax.ppermute(array, "blk", core_pairs)

    def across_chips(array, name, hop=2):
        with jax.named_scope(f"{name}_to_chip"):
            return lax.ppermute(array, ("shot", "blk"), chip_pairs(hop))

    def halos(array, name):
        return to_partner(array, name), across_chips(array, name)

    def in_hbm(array):
        return pltpu.with_memory_space_constraint(array, pltpu.HBM), HBM

    def to_owners(array, k, name):
        with jax.named_scope(f"{name}_to_{k}"):
            return lax.ppermute(array, "shot", [(i, i ^ k) for i in range(shots)])

    previous = state_before[0]
    present, later = adjoint_now[0], adjoint_later[0]

    wx, wy, wz, speed, current = call(
        "owner",
        owner_kernel,
        (piece,) * 4 + (field,),
        [in_hbm(a) for a in (epsilon, tilt_angle, azimuth, courant_sq, state_now)],
        (
            pltpu.VMEM((3, rows, count, depth), jnp.float32),
            pltpu.SemaphoreType.DMA((5,)),
        ),
    )
    first, wz_first = call(
        "first",
        first_kernel,
        (f32(8, depth), f32(rows + 1, count, depth)),
        [aperture_anchor, wz],
    )

    if shots == 4 and parts == 2:
        relay = functools.partial(relay_kernel, parts)
        wx_y = to_owners(wx, 2, "wx")
        wz_x = to_owners(wz_first, 1, "wz")
        wy_y = to_owners(wy, 2, "wy")
        wx_sent = call("relay_wx", relay, piece, [wz_x, wx, wx_y])
        wx_x = to_owners(wx_sent, 1, "wx")
        both = f32(2, rows, count, depth)
        wz_y = to_owners(call("pair_wz", pair_kernel, both, [wz, wz_x]), 2, "wz")
        wy_sent = call("relay_wy", relay, piece, [wz_x, wy, wy_y, wx_sent])
        wy_x = to_owners(wy_sent, 1, "wy")
        speed_x = to_owners(speed, 1, "speed")
        speed_y = to_owners(call("pair_speed", pair_kernel, both, [speed, speed_x]), 2, "speed")
        before = [wx_x, speed_x]
        pieces = [wx, wx_x, wx_y, wy, wy_x, wy_y, wz, wz_x, wz_y]
        places = [
            [(0, None), (1, None), (2, None), (1, None)],
            [(3, None), (4, None), (5, None), (4, None)],
            [(6, None), (7, slice(0, rows)), (8, 0), (8, 1)],
        ]
        speed_pieces = [speed, speed_x, speed_y]
        speed_places = [(0, None), (1, None), (2, 0), (2, 1)]
    else:
        pieces, places, before = [], [], []
        for array in (wx, wy, wz):
            places.append([(len(pieces) + k, None) for k in range(shots)])
            pieces = pieces + [array] + [to_owners(array, k, "w") for k in range(1, shots)]
        speed_places = places[0]
        speed_pieces = [speed] + [to_owners(speed, k, "speed") for k in range(1, shots)]

    now_p, now_a = to_partner(current, "state"), across_chips(current, "state", 1)
    slope, flags, matrix_y, matrix_z = call(
        "prepare",
        functools.partial(prepare_kernel, shots, parts),
        (
            f32(3, rows + 8, width, depth),
            f32(shots * parts, depth),
            jax.ShapeDtypeStruct((width, 2 * width), jnp.bfloat16),
            jax.ShapeDtypeStruct((2 * depth, depth), jnp.bfloat16),
        ),
        [first, current, now_p, now_a] + before,
        [wide],
    )
    edge = f32(3, 2, width, depth)
    tensor, flux, rest, *edges = call(
        "flux",
        functools.partial(flux_kernel, places, parts),
        (f32(3, rows, width, depth), field, field) + (edge,) * 4,
        [flags, slope, matrix_y, matrix_z] + pieces,
        flops=work // 3,
    )
    edges_a = [across_chips(a, "edge") for a in edges[:2]]
    edges_p = [to_partner(a, "edge") for a in edges[2:]]
    src, inj = call(
        "inject",
        inject_kernel,
        (f32(STEPS - 1, rows, width, depth), f32(STEPS, rows, width, depth)),
        [step_index, source_x, source_y, source_z, wavelet, receiver_x, receiver_y, receiver_z]
        + [residual_traces],
    )

    speed, operand = call(
        "speed",
        functools.partial(speed_kernel, speed_places, parts),
        (field, field),
        [flags, present] + speed_pieces,
    )
    op_p, op_a = halos(operand, "adjoint")

    image, following, coef = call(
        "forward0",
        forward_first,
        (field, field, f32(4, rows + 8, width, depth)),
        [tensor, *edges_p, *edges_a, slope, flux, rest]
        + [current, previous, speed, src],
        [extended],
        work // 4,
    )
    images = [image]
    previous, current = current, following
    adjoints = [present]
    known = None
    for t in range(STEPS - 1):
        now_p, now_a = halos(current, "state")
        back = STEPS - 1 - t
        ins = [operand, op_a, op_p, coef, matrix_y, matrix_z, present, later, inj, speed]
        outs = (field, field)
        if back == 1:
            ins = ins + [adjoints[1]] + images
            outs = (field, field, field)
        result = call(
            f"backward{t}", functools.partial(backward, back), outs, ins, scratch, work
        )
        later, present, operand = present, result[0], result[1]
        if back == 1:
            known = result[2]
        adjoints.append(present)
        op_p, op_a = halos(operand, "adjoint")
        if t < STEPS - 2:
            image, following = call(
                f"forward{t + 1}",
                functools.partial(forward, t + 1),
                (field, field),
                [current, now_a, now_p, coef, matrix_y, matrix_z, previous, speed, src],
                scratch,
                work,
            )
            images.append(image)
            previous, current = current, following

    chunks = call(
        "forward3",
        functools.partial(forward_last, parts),
        (piece,) * shots,
        [current, now_a, now_p, coef, matrix_y, matrix_z, known, adjoints[0], flags],
        scratch + (own_rows,),
        work,
    )
    received = [to_owners(chunks[k], k, "grad") for k in range(1, shots)]
    final, copied, done = call(
        "backward3",
        functools.partial(backward, 0),
        (field, field, f32(8, depth)),
        [operand, op_a, op_p, coef, matrix_y, matrix_z, present, later, inj],
        scratch,
        work,
    )
    model_grad = call("total", total_kernel, piece, [chunks[0]] + received + [done])
    return (copied[None], final[None], model_grad)


def solution(mesh):
    in_specs = (
        P("shot", "blk", None, None),
        P("shot", "blk", None, None),
        P("shot", "blk", None, None),
        P("shot", "blk", None, None),
        P("blk", "shot", None),
        P("blk", "shot", None),
        P("blk", "shot", None),
        P("blk", "shot", None),
        P("shot"),
        P(),
        P("shot", None),
        P("shot", None, None),
        P("shot"),
        P("shot"),
        P("shot"),
        P("shot", None),
        P("shot", None),
        P("shot", None),
    )
    out_specs = (P("shot", "blk", None, None), P("shot", "blk", None, None), P("blk", "shot", None))
    return jax.shard_map(
        on_device, mesh=mesh, in_specs=in_specs, out_specs=out_specs, check_vma=False
    )
```
